256 devices in a mesh: batch: 4 (over y), expert: 64 (over x, z, core).
Axes of the slice: x: 4, y: 4, z: 8, core: 2. Of those that a mesh axis runs over, the one named last changes fastest.
Arguments:
- tokens: bfloat16 [32768, 1024], P(('batch', 'expert')), may hold values from -6 to 6
- cotangent: bfloat16 [32768, 1024], P(('batch', 'expert')), may hold values from -6 to 6
- domain_ids: int32 [32768], P(('batch', 'expert')), may hold values from 0 to 7
- shared_ids: int32 [32768, 2], P(('batch', 'expert')), may hold values from 0 to 63, all different within a row
- private_ids: int32 [32768, 2], P(('batch', 'expert')), may hold values from 0 to 7, all different within a row
- gate_weight: bfloat16 [1024, 8, 72], replicated, may hold values from -0.375 to 0.375
- shared_in: bfloat16 [64, 1024, 2048], P('expert', None, 'batch'), may hold values from -0.1875 to 0.1875
- shared_out: bfloat16 [64, 2048, 1024], P('expert', 'batch'), may hold values from -0.125 to 0.125
- private_in: bfloat16 [64, 1024, 2048], P('expert', None, 'batch'), may hold values from -0.1875 to 0.1875
- private_out: bfloat16 [64, 2048, 1024], P('expert', 'batch'), may hold values from -0.125 to 0.125
Outputs:
- mixed: bfloat16 [32768, 1024], P(('batch', 'expert'))
- grad_shared_in: bfloat16 [64, 1024, 2048], P('expert', None, 'batch')
- grad_shared_out: bfloat16 [64, 2048, 1024], P('expert', 'batch')
- grad_private_in: bfloat16 [64, 1024, 2048], P('expert', None, 'batch')
- grad_private_out: bfloat16 [64, 2048, 1024], P('expert', 'batch')
- grad_gate: float32 [1024, 8, 72], P(('batch', 'expert'))
The draws below stay inside these ranges and needn't reach their ends.
All inputs are finite; a program needn't handle non-finite values.
Results may differ from the reference program's by a relative error of at most 0.015.
Values may be sent and summed in bfloat16 or wider, within the bound.
No kernel may reach another device: no remote copies, remote signals or barrier semaphores. Data moves between devices by JAX's collectives and lax.ppermute only.
A program may use at most 128 MiB of HBM per device.

```python
import math
import jax
import jax.numpy as jnp
import numpy as np
from jax import lax

D = 1024
HIDDEN_SIZE = 2048
SHARED = 64
PRIV = 8
DOMAINS = 8
TOK_DEV = 128
PRIVATE = 64
GATES = 72
CAP = 4
TOKENS = 32768
N_BATCH = 4


def with_ends(values, rng, low, largest):
    spot = [jax.random.randint(jax.random.fold_in(rng, axis), (), 0, length) for axis, length in enumerate(values.shape)]
    widest = values.shape.index(max(values.shape))
    next_to = spot[:widest] + [(spot[widest] + 1) % values.shape[widest]] + spot[widest + 1:]
    return values.at[tuple(spot)].set(low).at[tuple(next_to)].set(largest)


def levels(own_key, extent, shards, smallest, largest):
    def one(axis_at, blocks):
        heights = jax.random.uniform(jax.random.fold_in(jax.random.fold_in(own_key, 6), axis_at), (blocks,), jnp.float32, smallest / len(shards), largest / len(shards))
        return jnp.repeat(jnp.exp(heights), extent[axis_at] // blocks).reshape((-1,) + (1,) * (len(extent) - axis_at - 1))

    factor_of = one(*shards[0])
    for cut in shards[1:]:
        factor_of = factor_of * one(*cut)
    return factor_of


def cumulative_ranks(number_of, slope):
    loads = [(1 << 20) // math.isqrt(rank ** slope) + 1 for rank in range(1, number_of + 1)]
    scale = 1 + sum(loads) // (1 << 30)
    return np.cumsum(np.array([max(1, weight // scale) for weight in loads]))


def skewed_ids(key, shape, count, skew):
    table = cumulative_ranks(count, skew)
    lot = jax.random.randint(jax.random.fold_in(key, 1), shape, 0, int(table[count - 1]))
    rank = jnp.searchsorted(jnp.asarray(table, jnp.int32), lot, side="right")
    return jax.random.permutation(jax.random.fold_in(key, 2), count)[rank].astype(jnp.int32)


def different_ones(own_key, rows, amount, top, lift):
    order = jax.random.permutation(jax.random.fold_in(own_key, 1), amount)
    boost = order
    for power in range(3):
        boost = boost * boost // amount
    boost = boost * lift // amount
    chance = jax.random.randint(jax.random.fold_in(own_key, 2), (rows, amount), 0, 4096) + boost
    fixed_rows = jax.random.permutation(jax.random.fold_in(own_key, 3), rows)[jnp.arange(amount) % rows]
    chance = jnp.where(jnp.arange(rows)[:, None] == fixed_rows[None, :], 1 << 14, chance)
    score = chance * amount + jnp.arange(amount)
    return lax.top_k(score.astype(jnp.int32), top)[1].astype(jnp.int32)


def normal_values(key, dims, scale, reach, split=(), kind=jnp.bfloat16):
    array = jax.random.normal(key, dims, jnp.float32) * scale
    if len(split) > 0:
        array = levels(key, dims, split, -0.22, 0.18) * array
    return jnp.clip(array, min=-reach, max=reach).astype(kind)


def setup_inputs(seed: int = 0) -> dict:
    splits = jax.random.split(jax.random.key(seed), 11)
    tokens = normal_values(splits[0], (TOKENS, D), 1.0, 6.0, ((0, 256),))
    cotangent = normal_values(splits[1], (TOKENS, D), 1.0, 6.0, ((0, 256),))
    domain_ids = with_ends(skewed_ids(splits[2], (TOKENS,), DOMAINS, 2), jax.random.fold_in(splits[2], 3), 0, DOMAINS - 1).astype(jnp.int32)
    shared_ids = different_ones(splits[3], TOKENS, SHARED, 2, 256)
    private_ids = different_ones(splits[4], TOKENS, PRIV, 2, 2048)
    gate_weight = normal_values(splits[5], (D, DOMAINS, GATES), (D // 4) ** -0.5, 0.375)
    shared_in = normal_values(splits[6], (SHARED, D, HIDDEN_SIZE), D ** -0.5, 0.1875, ((0, 64), (2, 4)))
    shared_out = normal_values(splits[7], (SHARED, HIDDEN_SIZE, D), HIDDEN_SIZE ** -0.5, 0.125, ((0, 64), (1, 4)))
    private_in = normal_values(splits[8], (PRIVATE, D, HIDDEN_SIZE), D ** -0.5, 0.1875, ((0, 64), (2, 4)))
    private_out = normal_values(splits[9], (PRIVATE, HIDDEN_SIZE, D), HIDDEN_SIZE ** -0.5, 0.125, ((0, 64), (1, 4)))
    return {"tokens": tokens, "cotangent": cotangent, "domain_ids": domain_ids, "shared_ids": shared_ids, "private_ids": private_ids, "gate_weight": gate_weight, "shared_in": shared_in, "shared_out": shared_out, "private_in": private_in, "private_out": private_out}


def silu_slope(values):
    sigmoid = jax.nn.sigmoid(values)
    return sigmoid * (1.0 + values * (1.0 - sigmoid))


def block_slots(expert_ids, number):
    blocks = expert_ids.reshape(-1, TOK_DEV, 2)
    onehot = (blocks[..., None] == jnp.arange(number, dtype=jnp.int32)).astype(jnp.int32)
    per_row = jnp.sum(onehot, axis=2)
    earlier = jnp.cumsum(per_row, axis=1) - per_row
    return jnp.sum(onehot * earlier[:, :, None, :], axis=3).reshape(TOKENS, 2)


def grouped(values):
    return values.reshape(N_BATCH, -1, values.shape[-1]).astype(jnp.float32)


def expert_kind(mixed, tokens, cotangent, expert_ids, gates_kind, number, weight_in, weight_out):
    blocks = TOKENS // TOK_DEV
    slots = block_slots(expert_ids, number)
    source = (jnp.arange(TOKENS, dtype=jnp.int32) // TOK_DEV)[:, None]
    picks = jnp.arange(TOKENS * 2, dtype=jnp.int32).reshape(TOKENS, 2)
    places = jnp.where(slots < CAP, source * CAP + slots, blocks * CAP)
    index = jnp.full((number, blocks * CAP), -1, jnp.int32)
    index = index.at[expert_ids.reshape(-1), places.reshape(-1)].set(picks.reshape(-1), mode="drop")
    flat_gates = gates_kind.reshape(-1)
    dgate = jnp.zeros((TOKENS * 2,), jnp.float32)

    def one_expert(state, inputs):
        mixed, dgate = state
        slot_picks, weight_a, weight_b = inputs
        live = slot_picks >= 0
        safe = jnp.maximum(slot_picks, 0)
        row_ids = safe // 2
        inputs_x = jnp.where(live[:, None], tokens[row_ids], jnp.zeros((), jnp.bfloat16))
        cot_rows = jnp.where(live[:, None], cotangent[row_ids].astype(jnp.float32), jnp.float32(0.0))
        gate_rows = jnp.where(live, flat_gates[safe], jnp.float32(0.0))
        scaled = (gate_rows[:, None] * cot_rows).astype(jnp.bfloat16)
        pre = jnp.dot(inputs_x, weight_a, preferred_element_type=jnp.float32)
        act = jax.nn.silu(pre).astype(jnp.bfloat16)
        expert_out = jnp.dot(act, weight_b, preferred_element_type=jnp.float32).astype(jnp.bfloat16)
        out_float = expert_out.astype(jnp.float32)
        mixed = mixed.at[jnp.where(live, row_ids, TOKENS)].add(gate_rows[:, None] * out_float, mode="drop")
        dgate = dgate.at[jnp.where(live, safe, TOKENS * 2)].add(jnp.sum(cot_rows * out_float, axis=1), mode="drop")
        back = (jnp.dot(scaled, weight_b.T, preferred_element_type=jnp.float32) * silu_slope(pre)).astype(jnp.bfloat16)
        part_out = jnp.einsum("brh,brd->bhd", grouped(act), grouped(scaled)).astype(jnp.bfloat16)
        part_in = jnp.einsum("brd,brh->bdh", grouped(inputs_x), grouped(back)).astype(jnp.bfloat16)
        grad_b = jnp.sum(part_out.astype(jnp.float32), axis=0).astype(jnp.bfloat16)
        grad_a = jnp.sum(part_in.astype(jnp.float32), axis=0).astype(jnp.bfloat16)
        return (mixed, dgate), (grad_a, grad_b)

    (mixed, dgate), (grad_a, grad_b) = lax.scan(one_expert, (mixed, dgate), (index, weight_in, weight_out))
    return mixed, dgate.reshape(TOKENS, 2), grad_a, grad_b


def reference(tokens, cotangent, domain_ids, shared_ids, private_ids, gate_weight, shared_in, shared_out, private_in, private_out):
    table = jnp.dot(tokens, gate_weight.reshape(D, DOMAINS * GATES), preferred_element_type=jnp.float32)
    base = domain_ids[:, None] * GATES
    columns = jnp.concatenate([base + shared_ids, base + SHARED + private_ids], axis=1).astype(jnp.int32)
    logits = jnp.take_along_axis(table, columns, axis=1)
    gates = jax.nn.softmax(logits, axis=1)
    private_expert = (domain_ids[:, None] * PRIV + private_ids).astype(jnp.int32)
    mixed = jnp.zeros((TOKENS, D), jnp.float32)
    mixed, dgate_shared, grad_shared_in, grad_shared_out = expert_kind(mixed, tokens, cotangent, shared_ids, gates[:, 0:2], SHARED, shared_in, shared_out)
    mixed, dgate_private, grad_private_in, grad_private_out = expert_kind(mixed, tokens, cotangent, private_expert, gates[:, 2:4], PRIVATE, private_in, private_out)
    dgate = jnp.concatenate([dgate_shared, dgate_private], axis=1)
    dlogit = gates * (dgate - jnp.sum(gates * dgate, axis=1, keepdims=True))
    row_index = jnp.arange(TOKENS, dtype=jnp.int32)[:, None]
    spread = jnp.zeros((TOKENS, DOMAINS * GATES), jnp.float32).at[row_index, columns].add(dlogit)
    grad_gate = jnp.dot(tokens.astype(jnp.float32).T, spread, precision=lax.Precision.HIGHEST).reshape(D, DOMAINS, GATES)
    return mixed.astype(jnp.bfloat16), grad_shared_in, grad_shared_out, grad_private_in, grad_private_out, grad_gate
```

```python
import jax
import jax.numpy as jnp
from jax import lax
from jax.sharding import PartitionSpec as P

SHARED = 64
PRIV = 8
DOMAINS = 8
PRIVATE = 64
GATES = 72
CAP = 4
BF = jnp.bfloat16
F32 = jnp.float32


def turn(values, step):
    size = lax.axis_size("batch")
    return lax.ppermute(values, "batch", [(i, (i + step) % size) for i in range(size)])


def gather_ring(values):
    half = values.shape[0] // 2
    before = turn(values, 1)
    after = turn(values, -1)
    top = turn(before[:half], 1)
    bottom = turn(after[half:], -1)
    return [values, before, after, jnp.concatenate([top, bottom], axis=0)]


def scatter_ring(parts):
    own, before, after, far = parts
    half = own.shape[0] // 2
    top = turn(far[:half].astype(BF), 1)
    bottom = turn(far[half:].astype(BF), -1)
    after = jnp.concatenate([after[:half] + top.astype(F32), after[half:]], axis=0)
    before = jnp.concatenate([before[:half], before[half:] + bottom.astype(F32)], axis=0)
    right = turn(after.astype(BF), 1)
    left = turn(before.astype(BF), -1)
    return own + right.astype(F32) + left.astype(F32)


def cells_of(expert_ids, number, height):
    experts = jnp.arange(number, dtype=jnp.int32)
    onehot = (expert_ids[:, :, None] == experts[None, None, :]).astype(F32)
    per_row = jnp.sum(onehot, axis=1)
    order = jnp.arange(height, dtype=jnp.int32)
    lower = (order[:, None] > order[None, :]).astype(BF)
    earlier = jnp.dot(lower, per_row.astype(BF), preferred_element_type=F32)
    slots = jnp.sum(onehot * earlier[:, None, :], axis=2).astype(jnp.int32)
    target = jnp.where(slots < CAP, expert_ids * CAP + slots, -1)
    cells = jnp.arange(number * CAP, dtype=jnp.int32)
    return [cells[:, None] == target[None, :, pick] for pick in range(2)]


def exchange(values):
    return lax.all_to_all(values, "expert", split_axis=0, concat_axis=0, tiled=True)


def body(
    tokens,
    cotangent,
    domain_ids,
    shared_ids,
    private_ids,
    gate_weight,
    shared_in,
    shared_out,
    private_in,
    private_out,
):
    height, features = tokens.shape
    columns_all = DOMAINS * GATES
    n_batch = lax.axis_size("batch")
    me = lax.axis_index("batch")
    weights = ((shared_in[0], shared_out[0]), (private_in[0], private_out[0]))

    picks = (
        cells_of(shared_ids, SHARED, height),
        cells_of(domain_ids[:, None] * PRIV + private_ids, PRIVATE, height),
    )
    placed = [(pair[0] | pair[1]).astype(BF) for pair in picks]
    rows = []
    for kind in range(2):
        packed = jnp.dot(placed[kind], tokens, preferred_element_type=F32).astype(BF)
        got = exchange(packed.reshape(-1, CAP, features))
        rows.append(gather_ring(got.reshape(-1, features)))

    table = jnp.dot(
        tokens, gate_weight.reshape(features, columns_all), preferred_element_type=F32
    )
    base = domain_ids[:, None] * GATES
    columns = jnp.concatenate([base + shared_ids, base + SHARED + private_ids], axis=1)
    every = jnp.arange(columns_all, dtype=jnp.int32)
    logits = jnp.sum(
        jnp.where(columns[:, :, None] == every[None, None, :], table[:, None, :], 0.0), axis=2
    )
    gates = jax.nn.softmax(logits, axis=1)
    scaled = []
    for kind in range(2):
        first, second = picks[kind]
        weight = jnp.sum(
            jnp.where(first, gates[None, :, 2 * kind], 0.0)
            + jnp.where(second, gates[None, :, 2 * kind + 1], 0.0),
            axis=1,
            keepdims=True,
        )
        spot = jnp.dot(placed[kind], cotangent, preferred_element_type=F32)
        scaled.append((weight * spot).astype(BF))
    scaled = jnp.concatenate(scaled, axis=1).reshape(-1, CAP, 2 * features)
    scaled = exchange(scaled).reshape(-1, 2 * features)

    held = []
    partial = []
    for kind in range(2):
        weight_in, weight_out = weights[kind]
        group = []
        outs = []
        for block in rows[kind]:
            pre = jnp.dot(block, weight_in, preferred_element_type=F32)
            sigmoid = jax.nn.sigmoid(pre)
            act = (pre * sigmoid).astype(BF)
            slope = sigmoid * (1.0 + pre * (1.0 - sigmoid))
            outs.append(jnp.dot(act, weight_out, preferred_element_type=F32))
            group.append((act, slope))
        held.append(group)
        partial.append(outs)
    summed = jnp.concatenate([scatter_ring(outs).astype(BF) for outs in partial], axis=1)
    summed, scaled = lax.optimization_barrier((summed, scaled))
    scaled = gather_ring(scaled)
    returned = exchange(summed.reshape(-1, CAP, 2 * features))
    returned = returned.reshape(-1, 2 * features)

    cot_float = cotangent.astype(F32)
    mixed = jnp.zeros((height, features), F32)
    dgate = []
    for kind in range(2):
        flat = returned[:, kind * features : (kind + 1) * features]
        for pick in range(2):
            chosen = picks[kind][pick].astype(BF)
            output = lax.dot_general(
                chosen, flat, (((0,), (0,)), ((), ())), preferred_element_type=F32
            )
            number = 2 * kind + pick
            mixed = mixed + gates[:, number : number + 1] * output
            dgate.append(jnp.sum(cot_float * output, axis=1))
    dgate = jnp.stack(dgate, axis=1)
    dlogit = gates * (dgate - jnp.sum(gates * dgate, axis=1, keepdims=True))

    width = features // n_batch
    columns_t = columns.T
    dlogit_t = dlogit.T
    column_set = [columns_t]
    dlogit_set = [dlogit_t]
    token_set = [lax.dynamic_slice_in_dim(tokens, me * width, width, axis=1)]
    for step in range(1, n_batch):
        to = (me + step) % n_batch
        token_set.append(turn(lax.dynamic_slice_in_dim(tokens, to * width, width, axis=1), step))
        column_set.append(turn(columns_t, step))
        dlogit_set.append(turn(dlogit_t, step))
    token_part = jnp.concatenate(token_set, axis=0)
    column_part = jnp.concatenate(column_set, axis=1)
    dlogit_part = jnp.concatenate(dlogit_set, axis=1)
    spread = jnp.sum(
        jnp.where(
            column_part[:, None, :] == every[None, :, None], dlogit_part[:, None, :], 0.0
        ),
        axis=0,
    )
    term = lax.dot_general(
        token_part.astype(F32),
        spread,
        (((0,), (1,)), ((), ())),
        precision=lax.Precision.HIGHEST,
    )
    pieces = term.astype(BF).reshape(-1, features // (n_batch * lax.axis_size("expert")), columns_all)
    grad_gate = jnp.sum(exchange(pieces).astype(F32), axis=0).reshape(-1, DOMAINS, GATES)

    grads = []
    for kind in range(2):
        weight_in, weight_out = weights[kind]
        grad_in = 0.0
        grad_out = 0.0
        for block, (act, slope), sent in zip(rows[kind], held[kind], scaled):
            cot = sent[:, kind * features : (kind + 1) * features]
            back = lax.dot_general(
                cot, weight_out, (((1,), (1,)), ((), ())), preferred_element_type=F32
            )
            back = (back * slope).astype(BF)
            grad_out = grad_out + lax.dot_general(
                act, cot, (((0,), (0,)), ((), ())), preferred_element_type=F32
            )
            grad_in = grad_in + lax.dot_general(
                block, back, (((0,), (0,)), ((), ())), preferred_element_type=F32
            )
        grads.append(grad_in.astype(BF)[None])
        grads.append(grad_out.astype(BF)[None])
    return (mixed.astype(BF), grads[0], grads[1], grads[2], grads[3], grad_gate)


def solution(mesh):
    return jax.shard_map(
        body,
        mesh=mesh,
        in_specs=(
            P(("batch", "expert"), None),
            P(("batch", "expert"), None),
            P(("batch", "expert")),
            P(("batch", "expert"), None),
            P(("batch", "expert"), None),
            P(),
            P("expert", None, "batch"),
            P("expert", "batch", None),
            P("expert", None, "batch"),
            P("expert", "batch", None),
        ),
        out_specs=(
            P(("batch", "expert"), None),
            P("expert", None, "batch"),
            P("expert", "batch", None),
            P("expert", None, "batch"),
            P("expert", "batch", None),
            P(("batch", "expert"), None, None),
        ),
        check_vma=False,
    )
```

```python
import functools

import jax
import jax.numpy as jnp
from jax import lax
from jax.experimental import pallas as pl
from jax.experimental.pallas import tpu as pltpu
from jax.sharding import PartitionSpec as P

SHARED = 64
PRIV = 8
DOMAINS = 8
PRIVATE = 64
GATES = 72
CAP = 4
BF = jnp.bfloat16
F32 = jnp.float32


def turn(values, step):
    size = lax.axis_size("batch")
    return lax.ppermute(values, "batch", [(i, (i + step) % size) for i in range(size)])


def gather_ring(values):
    half = values.shape[0] // 2
    own = values[:half], values[half:]
    before_first = turn(own[0], 1)
    after_second = turn(own[1], -1)
    before_second = turn(own[1], 1)
    after_first = turn(own[0], -1)
    far = turn(before_first, 1), turn(after_second, -1)
    return own, (before_first, before_second, after_first, after_second), far


def plus(first, second):
    return (first.astype(F32) + second.astype(F32)).astype(BF)


def scatter_ring(own, near, far):
    before_first, before_second, after_first, after_second = near
    right_second = turn(after_second, 1)
    left_first = turn(before_first, -1)
    via_right = turn(far[0], 1)
    via_left = turn(far[1], -1)
    right_first = turn(plus(after_first, via_right), 1)
    left_second = turn(plus(before_second, via_left), -1)
    first = own[0].astype(F32) + right_first.astype(F32) + left_first.astype(F32)
    second = own[1].astype(F32) + right_second.astype(F32) + left_second.astype(F32)
    return jnp.concatenate([first, second], axis=0).astype(BF)


def of_shared(shape):
    return lax.broadcasted_iota(jnp.int32, shape, 0) % (2 * CAP) < CAP


def forward_kernel(blocks, *refs):
    in_s, in_p, out_s, out_p = refs[blocks : blocks + 4]
    for number in range(blocks):
        block = refs[number][...]
        pre_ref, part_ref = refs[blocks + 4 + 2 * number : blocks + 6 + 2 * number]
        mask = of_shared(pre_ref.shape)
        pre = jnp.where(
            mask,
            jnp.dot(block, in_s[...], preferred_element_type=F32),
            jnp.dot(block, in_p[...], preferred_element_type=F32),
        )
        pre_ref[...] = pre
        act = pre / (1.0 + jnp.exp(-pre))
        part = jnp.dot(jnp.where(mask, act, 0.0).astype(BF), out_s[...], preferred_element_type=F32)
        part = part + jnp.dot(
            jnp.where(mask, 0.0, act).astype(BF), out_p[...], preferred_element_type=F32
        )
        part_ref[...] = part.astype(BF)


def forward(rows, weights):
    blocks = len(rows)
    height, features = rows[0].shape
    hidden = weights[0].shape[1]
    results = pl.pallas_call(
        functools.partial(forward_kernel, blocks),
        out_shape=(
            jax.ShapeDtypeStruct((height, hidden), F32),
            jax.ShapeDtypeStruct((height, features), BF),
        )
        * blocks,
        compiler_params=pltpu.CompilerParams(vmem_limit_bytes=24 << 20),
        cost_estimate=pl.CostEstimate(
            flops=8 * blocks * height * features * hidden,
            bytes_accessed=8 * features * hidden + 4 * blocks * height * (features + hidden),
            transcendentals=blocks * height * hidden,
        ),
    )(*rows, *weights)
    return results[0::2], results[1::2]


TURNED = (((0,), (0,)), ((), ()))
TURNED_RIGHT = (((1,), (1,)), ((), ()))


def backward_kernel(blocks, *refs):
    rows, sent, pres = refs[:blocks], refs[blocks : 2 * blocks], refs[2 * blocks : 3 * blocks]
    out_s, out_p, grad_in_s, grad_out_s, grad_in_p, grad_out_p = refs[3 * blocks :]
    part = out_s.shape[0]
    total_in = 0.0
    total_out = 0.0
    for block, cot, pre_ref in zip(rows, sent, pres):
        pre = pre_ref[...]
        mask = of_shared(pre.shape)
        sigmoid = 1.0 / (1.0 + jnp.exp(-pre))
        act = pre * sigmoid
        slope = sigmoid * (1.0 + pre * (1.0 - sigmoid))
        back = jnp.where(
            mask,
            lax.dot_general(cot[...], out_s[...], TURNED_RIGHT, preferred_element_type=F32),
            lax.dot_general(cot[...], out_p[...], TURNED_RIGHT, preferred_element_type=F32),
        )
        back = back * slope
        acts = jnp.concatenate([jnp.where(mask, act, 0.0), jnp.where(mask, 0.0, act)], axis=1)
        backs = jnp.concatenate([jnp.where(mask, back, 0.0), jnp.where(mask, 0.0, back)], axis=1)
        total_out = total_out + lax.dot_general(
            acts.astype(BF), cot[...], TURNED, preferred_element_type=F32
        )
        total_in = total_in + lax.dot_general(
            block[...], backs.astype(BF), TURNED, preferred_element_type=F32
        )
    grad_in_s[0] = total_in[:, :part].astype(BF)
    grad_in_p[0] = total_in[:, part:].astype(BF)
    grad_out_s[0] = total_out[:part].astype(BF)
    grad_out_p[0] = total_out[part:].astype(BF)


def backward(rows, sent, pres, weight_out_s, weight_out_p):
    blocks = len(rows)
    hidden, features = weight_out_s.shape
    part = hidden // 2
    height = sum(block.shape[0] for block in rows)
    whole = [pl.BlockSpec(block.shape, lambda h: (0, 0)) for block in rows]
    tiles = [pl.BlockSpec((block.shape[0], part), lambda h: (0, h)) for block in rows]
    weight = pl.BlockSpec((part, features), lambda h: (h, 0))
    return pl.pallas_call(
        functools.partial(backward_kernel, blocks),
        grid=(hidden // part,),
        in_specs=whole + whole + tiles + [weight, weight],
        out_specs=(
            pl.BlockSpec((1, features, part), lambda h: (0, 0, h)),
            pl.BlockSpec((1, part, features), lambda h: (0, h, 0)),
        )
        * 2,
        out_shape=(
            jax.ShapeDtypeStruct((1, features, hidden), BF),
            jax.ShapeDtypeStruct((1, hidden, features), BF),
        )
        * 2,
        compiler_params=pltpu.CompilerParams(vmem_limit_bytes=56 << 20),
        cost_estimate=pl.CostEstimate(
            flops=12 * height * features * hidden,
            bytes_accessed=4 * height * (features + hidden) + 12 * features * hidden,
            transcendentals=2 * height * hidden,
        ),
    )(*rows, *sent, *pres, weight_out_s, weight_out_p)


def cells_of(expert_ids, number, height, first):
    experts = jnp.arange(number, dtype=jnp.int32)
    onehot = (expert_ids[:, :, None] == experts[None, None, :]).astype(F32)
    per_row = jnp.sum(onehot, axis=1)
    order = jnp.arange(height, dtype=jnp.int32)
    lower = (order[:, None] > order[None, :]).astype(BF)
    earlier = jnp.dot(lower, per_row.astype(BF), preferred_element_type=F32)
    slots = jnp.sum(onehot * earlier[:, None, :], axis=2).astype(jnp.int32)
    target = jnp.where(slots < CAP, expert_ids * (2 * CAP) + first + slots, -1)
    cells = jnp.arange(number * 2 * CAP, dtype=jnp.int32)
    return [cells[:, None] == target[None, :, pick] for pick in range(2)]


def exchange(values):
    return lax.all_to_all(values, "expert", split_axis=0, concat_axis=0, tiled=True)


def body(
    tokens,
    cotangent,
    domain_ids,
    shared_ids,
    private_ids,
    gate_weight,
    shared_in,
    shared_out,
    private_in,
    private_out,
):
    height, features = tokens.shape
    columns_all = DOMAINS * GATES
    n_batch = lax.axis_size("batch")
    me = lax.axis_index("batch")
    weights = (shared_in[0], private_in[0], shared_out[0], private_out[0])

    pairs = (
        cells_of(shared_ids, SHARED, height, 0),
        cells_of(domain_ids[:, None] * PRIV + private_ids, PRIVATE, height, CAP),
    )
    picks = [pair for both in pairs for pair in both]
    placed = (picks[0] | picks[1] | picks[2] | picks[3]).astype(BF)
    packed = jnp.dot(placed, tokens, preferred_element_type=F32).astype(BF)
    got = exchange(packed.reshape(-1, 2 * CAP, features))

    table = jnp.dot(
        tokens, gate_weight.reshape(features, columns_all), preferred_element_type=F32
    )
    base = domain_ids[:, None] * GATES
    columns = jnp.concatenate([base + shared_ids, base + SHARED + private_ids], axis=1)
    every = jnp.arange(columns_all, dtype=jnp.int32)
    logits = jnp.sum(
        jnp.where(columns[:, :, None] == every[None, None, :], table[:, None, :], 0.0), axis=2
    )
    gates = jax.nn.softmax(logits, axis=1)
    weight = sum(
        jnp.where(pick, gates[None, :, number], 0.0) for number, pick in enumerate(picks)
    )
    weight = jnp.sum(weight, axis=1, keepdims=True)
    spot = jnp.dot(placed, cotangent, preferred_element_type=F32)
    scaled = (weight * spot).astype(BF)

    width = features // n_batch
    columns_t = columns.T
    column_set = [columns_t]
    token_set = [lax.dynamic_slice_in_dim(tokens, me * width, width, axis=1)]
    for step in range(1, n_batch):
        to = (me + step) % n_batch
        token_set.append(turn(lax.dynamic_slice_in_dim(tokens, to * width, width, axis=1), step))
        column_set.append(turn(columns_t, step))
    token_part = jnp.concatenate(token_set, axis=0)
    column_part = jnp.concatenate(column_set, axis=1)

    got, scaled, gates, token_part, column_part = lax.optimization_barrier(
        (got, scaled, gates, token_part, column_part)
    )

    own, near, far = gather_ring(got.reshape(-1, features))
    pre_own, part_own = forward(own, weights)
    scaled, part_own = lax.optimization_barrier((scaled, part_own))
    scaled = exchange(scaled.reshape(-1, 2 * CAP, features)).reshape(-1, features)
    pre_near, part_near = forward(near, weights)
    pre_far, part_far = forward(far, weights)
    summed = scatter_ring(part_own, part_near, part_far)
    summed, scaled = lax.optimization_barrier((summed, scaled))
    returned = exchange(summed.reshape(-1, 2 * CAP, features)).reshape(-1, features)
    sent = gather_ring(scaled)

    cot_float = cotangent.astype(F32)
    mixed = jnp.zeros((height, features), F32)
    dgate = []
    for number, pick in enumerate(picks):
        output = lax.dot_general(
            pick.astype(BF), returned, TURNED, preferred_element_type=F32
        )
        mixed = mixed + gates[:, number : number + 1] * output
        dgate.append(jnp.sum(cot_float * output, axis=1))
    dgate = jnp.stack(dgate, axis=1)
    dlogit = gates * (dgate - jnp.sum(gates * dgate, axis=1, keepdims=True))

    dlogit_t = dlogit.T
    dlogit_set = [dlogit_t] + [turn(dlogit_t, step) for step in range(1, n_batch)]
    dlogit_part = jnp.concatenate(dlogit_set, axis=1)
    spread = jnp.sum(
        jnp.where(
            column_part[:, None, :] == every[None, :, None], dlogit_part[:, None, :], 0.0
        ),
        axis=0,
    )
    term = lax.dot_general(
        token_part.astype(F32),
        spread,
        (((0,), (1,)), ((), ())),
        precision=lax.Precision.HIGHEST,
    )
    pieces = term.astype(BF).reshape(-1, features // (n_batch * lax.axis_size("expert")), columns_all)
    grad_gate = jnp.sum(exchange(pieces).astype(F32), axis=0).reshape(-1, DOMAINS, GATES)

    rows = (*own, *near, *far)
    sent = (*sent[0], *sent[1], *sent[2])
    grads = backward(rows, sent, (*pre_own, *pre_near, *pre_far), weights[2], weights[3])
    return (mixed.astype(BF), *grads, grad_gate)


def solution(mesh):
    return jax.shard_map(
        body,
        mesh=mesh,
        in_specs=(
            P(("batch", "expert"), None),
            P(("batch", "expert"), None),
            P(("batch", "expert")),
            P(("batch", "expert"), None),
            P(("batch", "expert"), None),
            P(),
            P("expert", None, "batch"),
            P("expert", "batch", None),
            P("expert", None, "batch"),
            P("expert", "batch", None),
        ),
        out_specs=(
            P(("batch", "expert"), None),
            P("expert", None, "batch"),
            P("expert", "batch", None),
            P("expert", None, "batch"),
            P("expert", "batch", None),
            P(("batch", "expert"), None, None),
        ),
        check_vma=False,
    )
```

```python
import functools

import jax
import jax.numpy as jnp
from jax import lax
from jax.experimental import pallas as pl
from jax.experimental.pallas import tpu as pltpu
from jax.sharding import PartitionSpec as P

SHARED = 64
PRIV = 8
DOMAINS = 8
PRIVATE = 64
GATES = 72
CAP = 4
BF = jnp.bfloat16
F32 = jnp.float32


def turn(values, step):
    size = lax.axis_size("batch")
    return lax.ppermute(values, "batch", [(i, (i + step) % size) for i in range(size)])


def near_blocks(values):
    half = values.shape[0] // 2
    before_first = turn(values[:half], 1)
    after_second = turn(values[half:], -1)
    return before_first, turn(values[half:], 1), turn(values[:half], -1), after_second


def far_blocks(near):
    return turn(near[0], 1), turn(near[3], -1)


def plus(first, second):
    return (first.astype(F32) + second.astype(F32)).astype(BF)


def scatter_ring(own, near, far):
    before_first, before_second, after_first, after_second = near
    right_second = turn(after_second, 1)
    left_first = turn(before_first, -1)
    via_right = turn(far[0], 1)
    via_left = turn(far[1], -1)
    right_first = turn(plus(after_first, via_right), 1)
    left_second = turn(plus(before_second, via_left), -1)
    half = own.shape[0] // 2
    first = own[:half].astype(F32) + right_first.astype(F32) + left_first.astype(F32)
    second = own[half:].astype(F32) + right_second.astype(F32) + left_second.astype(F32)
    return jnp.concatenate([first, second], axis=0).astype(BF)


def of_shared(shape):
    return lax.broadcasted_iota(jnp.int32, shape, 0) % (2 * CAP) < CAP


def offsets_of(blocks):
    places = [0]
    for block in blocks:
        places.append(places[-1] + block.shape[0])
    return places


def forward_kernel(blocks, *refs):
    rows, weights = refs[:blocks], refs[blocks : blocks + 4]
    pre_out = refs[blocks + 4 : 2 * blocks + 4]
    part_out = refs[2 * blocks + 4 : 3 * blocks + 4]
    rows_held, pre_held, part_held, in_s, in_p, out_s, out_p, row_sem, weight_sem, out_sem = refs[
        3 * blocks + 4 :
    ]
    places = offsets_of(rows)
    held = (in_s, in_p, out_s, out_p)
    row_copies = [
        pltpu.make_async_copy(
            rows[n], rows_held.at[pl.ds(places[n], rows[n].shape[0]), :], row_sem.at[n]
        )
        for n in range(blocks)
    ]
    weight_copies = [
        pltpu.make_async_copy(weights[n], held[n], weight_sem.at[n]) for n in range(4)
    ]
    row_copies[0].start()
    for copy in weight_copies:
        copy.start()
    for copy in row_copies[1:]:
        copy.start()
    outs = []
    for n in range(blocks):
        where = pl.ds(places[n], rows[n].shape[0])
        outs.append(pltpu.make_async_copy(pre_held.at[where, :], pre_out[n], out_sem.at[2 * n]))
        outs.append(
            pltpu.make_async_copy(part_held.at[where, :], part_out[n], out_sem.at[2 * n + 1])
        )
    weight_copies[0].wait()
    weight_copies[1].wait()
    chunk = 512
    for start in range(0, places[-1], chunk):
        here = [n for n in range(blocks) if start <= places[n] < start + chunk]
        for n in here:
            row_copies[n].wait()
        block = rows_held[start : start + chunk, :]
        mask = of_shared((chunk, in_s.shape[1]))
        pre = jnp.where(
            mask,
            jnp.dot(block, in_s[...], preferred_element_type=F32),
            jnp.dot(block, in_p[...], preferred_element_type=F32),
        )
        pre_held[start : start + chunk, :] = pre
        for n in here:
            outs[2 * n].start()
        act = pre / (1.0 + jnp.exp(-pre))
        if start == 0:
            weight_copies[2].wait()
            weight_copies[3].wait()
        part = jnp.dot(jnp.where(mask, act, 0.0).astype(BF), out_s[...], preferred_element_type=F32)
        part = part + jnp.dot(
            jnp.where(mask, 0.0, act).astype(BF), out_p[...], preferred_element_type=F32
        )
        part_held[start : start + chunk, :] = part.astype(BF)
        for n in here:
            outs[2 * n + 1].start()
    for copy in outs:
        copy.wait()


def forward(rows, weights):
    blocks = len(rows)
    features, hidden = weights[0].shape
    height = sum(block.shape[0] for block in rows)
    results = pl.pallas_call(
        functools.partial(forward_kernel, blocks),
        in_specs=[pl.BlockSpec(memory_space=pl.ANY)] * (blocks + 4),
        out_specs=[pl.BlockSpec(memory_space=pl.ANY)] * (2 * blocks),
        out_shape=[jax.ShapeDtypeStruct((block.shape[0], hidden), F32) for block in rows]
        + [jax.ShapeDtypeStruct((block.shape[0], features), BF) for block in rows],
        scratch_shapes=[
            pltpu.VMEM((height, features), BF),
            pltpu.VMEM((height, hidden), F32),
            pltpu.VMEM((height, features), BF),
        ]
        + [pltpu.VMEM(weight.shape, BF) for weight in weights]
        + [
            pltpu.SemaphoreType.DMA((blocks,)),
            pltpu.SemaphoreType.DMA((4,)),
            pltpu.SemaphoreType.DMA((2 * blocks,)),
        ],
        compiler_params=pltpu.CompilerParams(vmem_limit_bytes=60 << 20),
        cost_estimate=pl.CostEstimate(
            flops=8 * height * features * hidden,
            bytes_accessed=8 * features * hidden + 4 * height * (features + hidden),
            transcendentals=height * hidden,
        ),
    )(*rows, *weights)
    return list(results[:blocks]), list(results[blocks:])


TURNED = (((0,), (0,)), ((), ()))
TURNED_RIGHT = (((1,), (1,)), ((), ()))


def backward_kernel(counts, *refs):
    ends = [sum(counts[:n]) for n in range(len(counts) + 1)]
    sources = [refs[ends[n] : ends[n + 1]] for n in range(len(counts))]
    grads = refs[ends[-1] : ends[-1] + 4]
    rows_held, pre_held, sent_held, out_s, out_p, acts, backs = refs[ends[-1] + 4 : ends[-1] + 11]
    grads_held = refs[ends[-1] + 11 : ends[-1] + 15]
    source_sem, weight_sem, grad_sem = refs[ends[-1] + 15 :]
    weight_copies = [
        pltpu.make_async_copy(sources[3][n], (out_s, out_p)[n], weight_sem.at[n]) for n in range(2)
    ]
    copies = []
    for blocks, held in zip(sources[:3], (rows_held, pre_held, sent_held)):
        places = offsets_of(blocks)
        for n, block in enumerate(blocks):
            where = pl.ds(places[n], block.shape[0])
            copies.append(
                (
                    places[n + 1],
                    pltpu.make_async_copy(block, held.at[where, :], source_sem.at[len(copies)]),
                )
            )
    copies.sort(key=lambda entry: entry[0])
    for copy in weight_copies:
        copy.start()
    for _, copy in copies:
        copy.start()
    for copy in weight_copies:
        copy.wait()
    hidden = out_s.shape[0]
    part = hidden // 2
    height = rows_held.shape[0]
    chunk = 512
    outs = []
    for h in range(2):
        own = slice(h * part, (h + 1) * part)
        for start in range(0, height, chunk):
            if h == 0:
                for end, copy in copies:
                    if start < end <= start + chunk:
                        copy.wait()
            here = slice(start, start + chunk)
            pre = pre_held[here, own]
            cot = sent_held[here, :]
            mask = of_shared(pre.shape)
            sigmoid = 1.0 / (1.0 + jnp.exp(-pre))
            act = pre * sigmoid
            slope = sigmoid * (1.0 + pre * (1.0 - sigmoid))
            back = jnp.where(
                mask,
                lax.dot_general(cot, out_s[own, :], TURNED_RIGHT, preferred_element_type=F32),
                lax.dot_general(cot, out_p[own, :], TURNED_RIGHT, preferred_element_type=F32),
            )
            back = back * slope
            acts[here, :part] = jnp.where(mask, act, 0.0).astype(BF)
            acts[here, part:] = jnp.where(mask, 0.0, act).astype(BF)
            backs[here, :part] = jnp.where(mask, back, 0.0).astype(BF)
            backs[here, part:] = jnp.where(mask, 0.0, back).astype(BF)
        total = lax.dot_general(acts[...], sent_held[...], TURNED, preferred_element_type=F32)
        for kind in range(2):
            held = grads_held[2 * kind + 1]
            held[own, :] = total[kind * part : (kind + 1) * part].astype(BF)
            where = pl.ds(h * part, part)
            outs.append(
                pltpu.make_async_copy(
                    held.at[where, :], grads[2 * kind + 1].at[0, where, :], grad_sem.at[len(outs)]
                )
            )
            outs[-1].start()
        total = lax.dot_general(rows_held[...], backs[...], TURNED, preferred_element_type=F32)
        for kind in range(2):
            held = grads_held[2 * kind]
            held[:, own] = total[:, kind * part : (kind + 1) * part].astype(BF)
            where = pl.ds(h * part, part)
            outs.append(
                pltpu.make_async_copy(
                    held.at[:, where], grads[2 * kind].at[0, :, where], grad_sem.at[len(outs)]
                )
            )
            outs[-1].start()
    for copy in outs:
        copy.wait()


def backward(rows, pres, sent, weight_out_s, weight_out_p):
    hidden, features = weight_out_s.shape
    height = sum(block.shape[0] for block in rows)
    counts = (len(rows), len(pres), len(sent), 2)
    shapes = ((features, hidden), (hidden, features)) * 2
    return pl.pallas_call(
        functools.partial(backward_kernel, counts),
        in_specs=[pl.BlockSpec(memory_space=pl.ANY)] * sum(counts),
        out_specs=[pl.BlockSpec(memory_space=pl.ANY)] * 4,
        out_shape=[jax.ShapeDtypeStruct((1,) + shape, BF) for shape in shapes],
        scratch_shapes=[
            pltpu.VMEM((height, features), BF),
            pltpu.VMEM((height, hidden), F32),
            pltpu.VMEM((height, features), BF),
            pltpu.VMEM((hidden, features), BF),
            pltpu.VMEM((hidden, features), BF),
            pltpu.VMEM((height, hidden), BF),
            pltpu.VMEM((height, hidden), BF),
        ]
        + [pltpu.VMEM(shape, BF) for shape in shapes]
        + [
            pltpu.SemaphoreType.DMA((sum(counts[:3]),)),
            pltpu.SemaphoreType.DMA((2,)),
            pltpu.SemaphoreType.DMA((8,)),
        ],
        compiler_params=pltpu.CompilerParams(vmem_limit_bytes=60 << 20),
        cost_estimate=pl.CostEstimate(
            flops=12 * height * features * hidden,
            bytes_accessed=4 * height * (features + hidden) + 12 * features * hidden,
            transcendentals=2 * height * hidden,
        ),
    )(*rows, *pres, *sent, weight_out_s, weight_out_p)


def pack_kernel(domain, shared, private, tokens, target_ref, packed_ref):
    height = tokens.shape[0]
    order = lax.broadcasted_iota(jnp.int32, (height, height), 0)
    ahead = (order < lax.broadcasted_iota(jnp.int32, (height, height), 1)).astype(F32).astype(BF)
    experts = lax.broadcasted_iota(jnp.int32, (SHARED, height), 0)
    cells = lax.broadcasted_iota(jnp.int32, (packed_ref.shape[0], height), 0)
    placed = jnp.zeros(cells.shape, F32)
    for kind in range(2):
        ids = shared[...] if kind == 0 else domain[...] * PRIV + private[...]
        onehot = [(ids[k : k + 1, :] == experts).astype(F32) for k in range(2)]
        both = (onehot[0] + onehot[1]).astype(BF)
        earlier = jnp.dot(both, ahead, preferred_element_type=F32)
        for k in range(2):
            slot = jnp.sum(onehot[k] * earlier, axis=0, keepdims=True).astype(jnp.int32)
            cell = ids[k : k + 1, :] * (2 * CAP) + kind * CAP + slot
            cell = jnp.where(slot < CAP, cell, -1)
            placed = placed + (cell == cells).astype(F32)
            target_ref[2 * kind + k : 2 * kind + k + 1, :] = cell
    packed_ref[...] = jnp.dot(
        placed.astype(BF), tokens[...], preferred_element_type=F32
    ).astype(BF)


def pack(domain_ids, shared_ids, private_ids, tokens):
    height, features = tokens.shape
    return pl.pallas_call(
        pack_kernel,
        out_shape=(
            jax.ShapeDtypeStruct((4, height), jnp.int32),
            jax.ShapeDtypeStruct((SHARED * 2 * CAP, features), BF),
        ),
    )(domain_ids[None, :], shared_ids.T, private_ids.T, tokens)


def unpack_kernel(target_ref, gates_ref, cot_ref, returned, mixed_ref, dlogit_ref):
    cells = lax.broadcasted_iota(jnp.int32, (cot_ref.shape[0], returned.shape[0]), 1)
    cot = cot_ref[...].astype(F32)
    gates = gates_ref[...]
    mixed = jnp.zeros(cot.shape, F32)
    dgate = []
    for k in range(4):
        chosen = (target_ref[:, k : k + 1] == cells).astype(F32).astype(BF)
        output = jnp.dot(chosen, returned[...], preferred_element_type=F32)
        mixed = mixed + gates[:, k : k + 1] * output
        dgate.append(jnp.sum(cot * output, axis=1, keepdims=True))
    mixed_ref[...] = mixed.astype(BF)
    mean = sum(gates[:, k : k + 1] * dgate[k] for k in range(4))
    lanes = lax.broadcasted_iota(jnp.int32, (cot.shape[0], 128), 1)
    spread = jnp.zeros(lanes.shape, F32)
    for k in range(4):
        spread = jnp.where(lanes == k, gates[:, k : k + 1] * (dgate[k] - mean), spread)
    dlogit_ref[...] = spread.T[:4, :]


def unpack(targets, gates, cotangent, returned):
    return pl.pallas_call(
        unpack_kernel,
        out_shape=(
            jax.ShapeDtypeStruct(cotangent.shape, BF),
            jax.ShapeDtypeStruct(gates.shape[::-1], F32),
        ),
    )(targets, gates, cotangent, returned)


def gate_kernel(columns, dlogits, tokens, term_ref):
    wide = lax.broadcasted_iota(jnp.int32, (term_ref.shape[1], columns.shape[1]), 0)
    spread = jnp.zeros(wide.shape, F32)
    for k in range(4):
        spread = spread + jnp.where(columns[k : k + 1, :] == wide, dlogits[k : k + 1, :], 0.0)
    total = 0.0
    for _ in range(3):
        piece = spread.astype(BF)
        spread = spread - piece.astype(F32)
        total = total + lax.dot_general(
            tokens[...], piece, TURNED_RIGHT, preferred_element_type=F32
        )
    term_ref[...] = total.astype(BF)


def gate_term(columns, dlogits, tokens, width):
    return pl.pallas_call(
        gate_kernel,
        out_shape=jax.ShapeDtypeStruct((tokens.shape[0], width), BF),
    )(columns, dlogits, tokens)


def exchange(values):
    return lax.all_to_all(values, "expert", split_axis=0, concat_axis=0, tiled=True)


def body(
    tokens,
    cotangent,
    domain_ids,
    shared_ids,
    private_ids,
    gate_weight,
    shared_in,
    shared_out,
    private_in,
    private_out,
):
    height, features = tokens.shape
    columns_all = DOMAINS * GATES
    n_batch = lax.axis_size("batch")
    me = lax.axis_index("batch")
    weights = (shared_in[0], private_in[0], shared_out[0], private_out[0])

    targets, packed = pack(domain_ids, shared_ids, private_ids, tokens)
    got = exchange(packed.reshape(-1, 2 * CAP, features))
    cells = jnp.arange(packed.shape[0], dtype=jnp.int32)
    picks = [cells[:, None] == targets[None, k, :] for k in range(4)]
    placed = (picks[0] | picks[1] | picks[2] | picks[3]).astype(BF)

    table = jnp.dot(
        tokens, gate_weight.reshape(features, columns_all), preferred_element_type=F32
    )
    base = domain_ids[:, None] * GATES
    columns = jnp.concatenate([base + shared_ids, base + SHARED + private_ids], axis=1)
    every = jnp.arange(columns_all, dtype=jnp.int32)
    logits = jnp.sum(
        jnp.where(columns[:, :, None] == every[None, None, :], table[:, None, :], 0.0), axis=2
    )
    gates = jax.nn.softmax(logits, axis=1)
    weight = sum(
        jnp.where(pick, gates[None, :, number], 0.0) for number, pick in enumerate(picks)
    )
    weight = jnp.sum(weight, axis=1, keepdims=True)
    spot = jnp.dot(placed, cotangent, preferred_element_type=F32)
    scaled = (weight * spot).astype(BF)

    width = features // n_batch
    columns_t = columns.T
    column_set = [columns_t]
    token_set = [lax.dynamic_slice_in_dim(tokens, me * width, width, axis=1)]
    for step in range(1, n_batch):
        to = (me + step) % n_batch
        token_set.append(turn(lax.dynamic_slice_in_dim(tokens, to * width, width, axis=1), step))
        column_set.append(turn(columns_t, step))
    token_part = jnp.concatenate(token_set, axis=0).T
    column_part = jnp.concatenate(column_set, axis=1)

    got, scaled, gates, targets, token_part, column_part = lax.optimization_barrier(
        (got, scaled, gates, targets.T, token_part, column_part)
    )

    got = got.reshape(-1, features)
    near = list(near_blocks(got))
    pre_own, part_own = forward((got,), weights)
    scaled, near[0], near[3], part_own[0] = lax.optimization_barrier(
        (scaled, near[0], near[3], part_own[0])
    )
    far = far_blocks(near)
    scaled = exchange(scaled.reshape(-1, 2 * CAP, features)).reshape(-1, features)
    pre_far, part_far = forward(far, weights)
    pre_near, part_near = forward(near, weights)
    summed = scatter_ring(part_own[0], part_near, part_far)
    summed, scaled = lax.optimization_barrier((summed, scaled))
    returned = exchange(summed.reshape(-1, 2 * CAP, features)).reshape(-1, features)
    sent_near = near_blocks(scaled)
    returned, *sent_near = lax.optimization_barrier((returned, *sent_near))
    sent = (scaled, *sent_near, *far_blocks(sent_near))

    mixed, dlogit = unpack(targets, gates, cotangent, returned)

    dlogit_set = [dlogit] + [turn(dlogit, step) for step in range(1, n_batch)]
    dlogit_part = jnp.concatenate(dlogit_set, axis=1)
    term = gate_term(column_part, dlogit_part, token_part, columns_all)
    pieces = term.reshape(-1, features // (n_batch * lax.axis_size("expert")), columns_all)
    grad_gate = jnp.sum(exchange(pieces).astype(F32), axis=0).reshape(-1, DOMAINS, GATES)

    grads = backward(
        (got, *near, *far), (*pre_own, *pre_near, *pre_far), sent, shared_out[0], private_out[0]
    )
    return (mixed, *grads, grad_gate)


def solution(mesh):
    return jax.shard_map(
        body,
        mesh=mesh,
        in_specs=(
            P(("batch", "expert"), None),
            P(("batch", "expert"), None),
            P(("batch", "expert")),
            P(("batch", "expert"), None),
            P(("batch", "expert"), None),
            P(),
            P("expert", None, "batch"),
            P("expert", "batch", None),
            P("expert", None, "batch"),
            P("expert", "batch", None),
        ),
        out_specs=(
            P(("batch", "expert"), None),
            P("expert", None, "batch"),
            P("expert", "batch", None),
            P("expert", None, "batch"),
            P("expert", "batch", None),
            P(("batch", "expert"), None, None),
        ),
        check_vma=False,
    )
```

```python
import functools

import jax
import jax.numpy as jnp
from jax import lax
from jax.experimental import pallas as pl
from jax.experimental.pallas import tpu as pltpu
from jax.sharding import PartitionSpec as P

SHARED = 64
PRIV = 8
DOMAINS = 8
PRIVATE = 64
GATES = 72
CAP = 4
BF = jnp.bfloat16
F32 = jnp.float32


TURNED = (((0,), (0,)), ((), ()))
TURNED_RIGHT = (((1,), (1,)), ((), ()))


def turn(values, step):
    size = lax.axis_size("batch")
    return lax.ppermute(values, "batch", [(i, (i + step) % size) for i in range(size)])


def near_blocks(pair):
    before_shared = turn(pair[0], 1)
    after_private = turn(pair[1], -1)
    return [before_shared, turn(pair[1], 1), turn(pair[0], -1), after_private]


def far_blocks(near):
    return [turn(near[0], 1), turn(near[3], -1)]


def plus(first, second):
    return (first.astype(F32) + second.astype(F32)).astype(BF)


def scatter_ring(own, near, far):
    before_shared, before_private, after_shared, after_private = near
    via_right = turn(far[0], 1)
    via_left = turn(far[1], -1)
    right_private = turn(after_private, 1)
    left_shared = turn(before_shared, -1)
    right_shared = turn(plus(after_shared, via_right), 1)
    left_private = turn(plus(before_private, via_left), -1)
    return by_peer(own[0], right_shared, left_shared, own[1], right_private, left_private)


SPAN = 128


def chosen_rows(kind):
    row = lax.broadcasted_iota(jnp.int32, (SPAN, 2 * SPAN), 0)
    mixed = lax.broadcasted_iota(jnp.int32, (SPAN, 2 * SPAN), 1)
    place = row // CAP * (2 * CAP) + kind * CAP + row % CAP
    return (place == mixed).astype(F32).astype(BF)


def by_kind_kernel(values, *results):
    for kind, result in enumerate(results):
        chosen = chosen_rows(kind)
        for start in range(0, result.shape[0], SPAN):
            result[start : start + SPAN, :] = jnp.dot(
                chosen, values[2 * start : 2 * start + 2 * SPAN, :], preferred_element_type=F32
            ).astype(BF)


def by_kind(values):
    height, features = values.shape
    return list(
        pl.pallas_call(
            by_kind_kernel,
            out_shape=[jax.ShapeDtypeStruct((height // 2, features), BF)] * 2,
            compiler_params=pltpu.CompilerParams(vmem_limit_bytes=16 << 20),
        )(values)
    )


def by_peer_kernel(*refs):
    result = refs[-1]
    for start in range(0, result.shape[0], 2 * SPAN):
        total = 0.0
        for kind in range(2):
            here = slice(start // 2, start // 2 + SPAN)
            parts = [ref[here, :].astype(F32) for ref in refs[3 * kind : 3 * kind + 3]]
            total = total + lax.dot_general(
                chosen_rows(kind),
                (parts[0] + parts[1] + parts[2]).astype(BF),
                TURNED,
                preferred_element_type=F32,
            )
        result[start : start + 2 * SPAN, :] = total.astype(BF)


def by_peer(*parts):
    height, features = parts[0].shape
    return pl.pallas_call(
        by_peer_kernel,
        out_shape=jax.ShapeDtypeStruct((2 * height, features), BF),
        compiler_params=pltpu.CompilerParams(vmem_limit_bytes=16 << 20),
    )(*parts)


def forward_kernel(kinds, *refs):
    blocks = len(kinds)
    rows, weights = refs[:blocks], refs[blocks : blocks + 4]
    pre_out = refs[blocks + 4 : 2 * blocks + 4]
    part_out = refs[2 * blocks + 4 : 3 * blocks + 4]
    rows_held, pre_held, part_held, ins, outs, row_sem, weight_sem, out_sem = refs[3 * blocks + 4 :]
    row_copies = [
        pltpu.make_async_copy(rows[n], rows_held.at[n], row_sem.at[n]) for n in range(blocks)
    ]
    in_copies = [pltpu.make_async_copy(weights[n], ins.at[n], weight_sem.at[n]) for n in range(2)]
    out_copies = [
        pltpu.make_async_copy(weights[2 + n], outs.at[n], weight_sem.at[2 + n]) for n in range(2)
    ]
    for copy in (row_copies[0], in_copies[kinds[0]], out_copies[kinds[0]]):
        copy.start()
    for copy in row_copies[1:]:
        copy.start()
    for copy in (in_copies[1 - kinds[0]], out_copies[1 - kinds[0]]):
        copy.start()
    results = []
    seen = set()
    for n, kind in enumerate(kinds):
        row_copies[n].wait()
        if kind not in seen:
            in_copies[kind].wait()
        pre = jnp.dot(rows_held[n], ins[kind], preferred_element_type=F32)
        pre_held[n] = pre
        results.append(pltpu.make_async_copy(pre_held.at[n], pre_out[n], out_sem.at[2 * n]))
        results[-1].start()
        act = pre / (1.0 + jnp.exp(-pre))
        if kind not in seen:
            out_copies[kind].wait()
        seen.add(kind)
        part = jnp.dot(act.astype(BF), outs[kind], preferred_element_type=F32)
        part_held[n] = part.astype(BF)
        results.append(pltpu.make_async_copy(part_held.at[n], part_out[n], out_sem.at[2 * n + 1]))
        results[-1].start()
    for copy in results:
        copy.wait()


def forward(rows, kinds, weights):
    blocks = len(rows)
    features, hidden = weights[0].shape
    height = rows[0].shape[0]
    results = pl.pallas_call(
        functools.partial(forward_kernel, kinds),
        in_specs=[pl.BlockSpec(memory_space=pl.ANY)] * (blocks + 4),
        out_specs=[pl.BlockSpec(memory_space=pl.ANY)] * (2 * blocks),
        out_shape=[jax.ShapeDtypeStruct((height, hidden), F32)] * blocks
        + [jax.ShapeDtypeStruct((height, features), BF)] * blocks,
        scratch_shapes=[
            pltpu.VMEM((blocks, height, features), BF),
            pltpu.VMEM((blocks, height, hidden), F32),
            pltpu.VMEM((blocks, height, features), BF),
            pltpu.VMEM((2, features, hidden), BF),
            pltpu.VMEM((2, hidden, features), BF),
            pltpu.SemaphoreType.DMA((blocks,)),
            pltpu.SemaphoreType.DMA((4,)),
            pltpu.SemaphoreType.DMA((2 * blocks,)),
        ],
        compiler_params=pltpu.CompilerParams(vmem_limit_bytes=60 << 20),
        cost_estimate=pl.CostEstimate(
            flops=4 * blocks * height * features * hidden,
            bytes_accessed=8 * features * hidden + 4 * blocks * height * (features + hidden),
            transcendentals=blocks * height * hidden,
        ),
    )(*rows, *weights)
    return list(results[:blocks]), list(results[blocks:])


def backward_kernel(blocks, *refs):
    total = 2 * blocks
    rows, pres, sent = refs[:total], refs[total : 2 * total], refs[2 * total : 3 * total]
    weights, grads = refs[3 * total : 3 * total + 2], refs[3 * total + 2 : 3 * total + 6]
    rows_held, pre_held, sent_held, outs, acts, backs = refs[3 * total + 6 : 3 * total + 12]
    grads_held = refs[3 * total + 12 : 3 * total + 16]
    source_sem, weight_sem, grad_sem = refs[3 * total + 16 :]
    height = rows[0].shape[0]
    weight_copies = [
        pltpu.make_async_copy(weights[kind], outs.at[kind], weight_sem.at[kind])
        for kind in range(2)
    ]
    copies = []
    for kind in range(2):
        weight_copies[kind].start()
        for n in range(blocks):
            block = kind * blocks + n
            where = pl.ds(n * height, height)
            trio = [
                pltpu.make_async_copy(
                    source[block], held.at[kind, where, :], source_sem.at[3 * block + number]
                )
                for number, (source, held) in enumerate(
                    ((sent, sent_held), (pres, pre_held), (rows, rows_held))
                )
            ]
            for copy in trio:
                copy.start()
            copies.append(trio)
    results = []
    for kind in range(2):
        weight_copies[kind].wait()
        for n in range(blocks):
            for copy in copies[kind * blocks + n]:
                copy.wait()
            here = slice(n * height, (n + 1) * height)
            pre = pre_held[kind, here, :]
            sigmoid = 1.0 / (1.0 + jnp.exp(-pre))
            slope = sigmoid * (1.0 + pre * (1.0 - sigmoid))
            back = lax.dot_general(
                sent_held[kind, here, :], outs[kind], TURNED_RIGHT, preferred_element_type=F32
            )
            acts[here, :] = (pre * sigmoid).astype(BF)
            backs[here, :] = (back * slope).astype(BF)
        grads_held[2 * kind + 1][...] = lax.dot_general(
            acts[...], sent_held[kind], TURNED, preferred_element_type=F32
        ).astype(BF)
        results.append(
            pltpu.make_async_copy(
                grads_held[2 * kind + 1], grads[2 * kind + 1].at[0], grad_sem.at[2 * kind + 1]
            )
        )
        results[-1].start()
        grads_held[2 * kind][...] = lax.dot_general(
            rows_held[kind], backs[...], TURNED, preferred_element_type=F32
        ).astype(BF)
        results.append(
            pltpu.make_async_copy(grads_held[2 * kind], grads[2 * kind].at[0], grad_sem.at[2 * kind])
        )
        results[-1].start()
    for copy in results:
        copy.wait()


def backward(rows, pres, sent, weight_out_s, weight_out_p):
    hidden, features = weight_out_s.shape
    blocks = len(rows) // 2
    height = blocks * rows[0].shape[0]
    shapes = ((features, hidden), (hidden, features)) * 2
    return pl.pallas_call(
        functools.partial(backward_kernel, blocks),
        in_specs=[pl.BlockSpec(memory_space=pl.ANY)] * (6 * blocks + 2),
        out_specs=[pl.BlockSpec(memory_space=pl.ANY)] * 4,
        out_shape=[jax.ShapeDtypeStruct((1,) + shape, BF) for shape in shapes],
        scratch_shapes=[
            pltpu.VMEM((2, height, features), BF),
            pltpu.VMEM((2, height, hidden), F32),
            pltpu.VMEM((2, height, features), BF),
            pltpu.VMEM((2, hidden, features), BF),
            pltpu.VMEM((height, hidden), BF),
            pltpu.VMEM((height, hidden), BF),
        ]
        + [pltpu.VMEM(shape, BF) for shape in shapes]
        + [
            pltpu.SemaphoreType.DMA((6 * blocks,)),
            pltpu.SemaphoreType.DMA((2,)),
            pltpu.SemaphoreType.DMA((4,)),
        ],
        compiler_params=pltpu.CompilerParams(vmem_limit_bytes=60 << 20),
        cost_estimate=pl.CostEstimate(
            flops=12 * height * features * hidden,
            bytes_accessed=8 * height * (features + hidden) + 12 * features * hidden,
            transcendentals=2 * height * hidden,
        ),
    )(*rows, *pres, *sent, weight_out_s, weight_out_p)


def pack_kernel(domain, shared, private, tokens, target_ref, packed_ref):
    height = tokens.shape[0]
    order = lax.broadcasted_iota(jnp.int32, (height, height), 0)
    ahead = (order < lax.broadcasted_iota(jnp.int32, (height, height), 1)).astype(F32).astype(BF)
    experts = lax.broadcasted_iota(jnp.int32, (SHARED, height), 0)
    cells = lax.broadcasted_iota(jnp.int32, (packed_ref.shape[0], height), 0)
    placed = jnp.zeros(cells.shape, F32)
    for kind in range(2):
        ids = shared[...] if kind == 0 else domain[...] * PRIV + private[...]
        onehot = [(ids[k : k + 1, :] == experts).astype(F32) for k in range(2)]
        both = (onehot[0] + onehot[1]).astype(BF)
        earlier = jnp.dot(both, ahead, preferred_element_type=F32)
        for k in range(2):
            slot = jnp.sum(onehot[k] * earlier, axis=0, keepdims=True).astype(jnp.int32)
            cell = ids[k : k + 1, :] * (2 * CAP) + kind * CAP + slot
            cell = jnp.where(slot < CAP, cell, -1)
            placed = placed + (cell == cells).astype(F32)
            target_ref[2 * kind + k : 2 * kind + k + 1, :] = cell
    packed_ref[...] = jnp.dot(
        placed.astype(BF), tokens[...], preferred_element_type=F32
    ).astype(BF)


def pack(domain_ids, shared_ids, private_ids, tokens):
    height, features = tokens.shape
    return pl.pallas_call(
        pack_kernel,
        out_shape=(
            jax.ShapeDtypeStruct((4, height), jnp.int32),
            jax.ShapeDtypeStruct((SHARED * 2 * CAP, features), BF),
        ),
    )(domain_ids[None, :], shared_ids.T, private_ids.T, tokens)


def unpack_kernel(target_ref, gates_ref, cot_ref, returned, mixed_ref, dlogit_ref):
    cells = lax.broadcasted_iota(jnp.int32, (cot_ref.shape[0], returned.shape[0]), 1)
    cot = cot_ref[...].astype(F32)
    gates = gates_ref[...]
    mixed = jnp.zeros(cot.shape, F32)
    dgate = []
    for k in range(4):
        chosen = (target_ref[:, k : k + 1] == cells).astype(F32).astype(BF)
        output = jnp.dot(chosen, returned[...], preferred_element_type=F32)
        mixed = mixed + gates[:, k : k + 1] * output
        dgate.append(jnp.sum(cot * output, axis=1, keepdims=True))
    mixed_ref[...] = mixed.astype(BF)
    mean = sum(gates[:, k : k + 1] * dgate[k] for k in range(4))
    lanes = lax.broadcasted_iota(jnp.int32, (cot.shape[0], 128), 1)
    spread = jnp.zeros(lanes.shape, F32)
    for k in range(4):
        spread = jnp.where(lanes == k, gates[:, k : k + 1] * (dgate[k] - mean), spread)
    dlogit_ref[...] = spread.T[:4, :]


def unpack(targets, gates, cotangent, returned):
    return pl.pallas_call(
        unpack_kernel,
        out_shape=(
            jax.ShapeDtypeStruct(cotangent.shape, BF),
            jax.ShapeDtypeStruct(gates.shape[::-1], F32),
        ),
    )(targets, gates, cotangent, returned)


def gate_kernel(columns, dlogits, tokens, term_ref):
    wide = lax.broadcasted_iota(jnp.int32, (term_ref.shape[1], columns.shape[1]), 0)
    spread = jnp.zeros(wide.shape, F32)
    for k in range(4):
        spread = spread + jnp.where(columns[k : k + 1, :] == wide, dlogits[k : k + 1, :], 0.0)
    total = 0.0
    for _ in range(3):
        piece = spread.astype(BF)
        spread = spread - piece.astype(F32)
        total = total + lax.dot_general(
            tokens[...], piece, TURNED_RIGHT, preferred_element_type=F32
        )
    term_ref[...] = total.astype(BF)


def gate_term(columns, dlogits, tokens, width):
    return pl.pallas_call(
        gate_kernel,
        out_shape=jax.ShapeDtypeStruct((tokens.shape[0], width), BF),
    )(columns, dlogits, tokens)


def exchange(values):
    return lax.all_to_all(values, "expert", split_axis=0, concat_axis=0, tiled=True)


def body(
    tokens,
    cotangent,
    domain_ids,
    shared_ids,
    private_ids,
    gate_weight,
    shared_in,
    shared_out,
    private_in,
    private_out,
):
    height, features = tokens.shape
    columns_all = DOMAINS * GATES
    n_batch = lax.axis_size("batch")
    me = lax.axis_index("batch")
    weights = (shared_in[0], private_in[0], shared_out[0], private_out[0])

    targets, packed = pack(domain_ids, shared_ids, private_ids, tokens)
    base = domain_ids[:, None] * GATES
    columns = jnp.concatenate([base + shared_ids, base + SHARED + private_ids], axis=1)
    targets, packed, tokens = lax.optimization_barrier((targets, packed, tokens))
    got = exchange(packed.reshape(-1, 2 * CAP, features))
    cells = jnp.arange(packed.shape[0], dtype=jnp.int32)
    picks = [cells[:, None] == targets[None, k, :] for k in range(4)]
    placed = (picks[0] | picks[1] | picks[2] | picks[3]).astype(BF)

    table = jnp.dot(
        tokens, gate_weight.reshape(features, columns_all), preferred_element_type=F32
    )
    every = jnp.arange(columns_all, dtype=jnp.int32)
    logits = jnp.sum(
        jnp.where(columns[:, :, None] == every[None, None, :], table[:, None, :], 0.0), axis=2
    )
    gates = jax.nn.softmax(logits, axis=1)
    columns, gates = lax.optimization_barrier((columns, gates))
    weight = sum(
        jnp.where(pick, gates[None, :, number], 0.0) for number, pick in enumerate(picks)
    )
    weight = jnp.sum(weight, axis=1, keepdims=True)
    spot = jnp.dot(placed, cotangent, preferred_element_type=F32)
    scaled = (weight * spot).astype(BF)

    width = features // n_batch
    columns_t = columns.T
    column_set = [columns_t]
    token_set = [lax.dynamic_slice_in_dim(tokens, me * width, width, axis=1)]
    for step in range(1, n_batch):
        to = (me + step) % n_batch
        token_set.append(turn(lax.dynamic_slice_in_dim(tokens, to * width, width, axis=1), step))
        column_set.append(turn(columns_t, step))
    token_part = jnp.concatenate(token_set, axis=0).T
    column_part = jnp.concatenate(column_set, axis=1)

    got, scaled, gates, targets, token_part, column_part = lax.optimization_barrier(
        (got, scaled, gates, targets.T, token_part, column_part)
    )

    own = by_kind(got.reshape(-1, features))
    near = near_blocks(own)
    pre_own, part_own = forward(own, (0, 1), weights)
    near[0], near[3], part_own[0] = lax.optimization_barrier((near[0], near[3], part_own[0]))
    far = far_blocks(near)
    pre_first, part_first = forward((near[0], near[3]), (0, 1), weights)
    scaled, part_first[0] = lax.optimization_barrier((scaled, part_first[0]))
    scaled = exchange(scaled.reshape(-1, 2 * CAP, features))
    pre_far, part_far = forward(far, (0, 1), weights)
    pre_second, part_second = forward((near[1], near[2]), (1, 0), weights)
    part_near = (part_first[0], part_second[0], part_second[1], part_first[1])
    pre_near = (pre_first[0], pre_second[0], pre_second[1], pre_first[1])
    summed = scatter_ring(part_own, part_near, part_far)
    summed, scaled = lax.optimization_barrier((summed, scaled))
    returned = exchange(summed.reshape(-1, 2 * CAP, features)).reshape(-1, features)
    sent_own = by_kind(scaled.reshape(-1, features))
    sent_near = near_blocks(sent_own)
    returned, *sent_near = lax.optimization_barrier((returned, *sent_near))

    mixed, dlogit = unpack(targets, gates, cotangent, returned)

    dlogit_set = [dlogit] + [turn(dlogit, step) for step in range(1, n_batch)]
    dlogit_part = jnp.concatenate(dlogit_set, axis=1)
    dlogit_part, sent_near[0], sent_near[3] = lax.optimization_barrier(
        (dlogit_part, sent_near[0], sent_near[3])
    )
    sent_far = far_blocks(sent_near)
    term = gate_term(column_part, dlogit_part, token_part, columns_all)
    pieces = term.reshape(-1, features // (n_batch * lax.axis_size("expert")), columns_all)
    grad_gate = jnp.sum(exchange(pieces).astype(F32), axis=0).reshape(-1, DOMAINS, GATES)

    ordered = [
        (o[0], n[0], n[2], f[0], o[1], n[1], n[3], f[1])
        for o, n, f in (
            (own, near, far),
            (pre_own, pre_near, pre_far),
            (sent_own, sent_near, sent_far),
        )
    ]
    grads = backward(*ordered, shared_out[0], private_out[0])
    return (mixed, *grads, grad_gate)


def solution(mesh):
    return jax.shard_map(
        body,
        mesh=mesh,
        in_specs=(
            P(("batch", "expert"), None),
            P(("batch", "expert"), None),
            P(("batch", "expert")),
            P(("batch", "expert"), None),
            P(("batch", "expert"), None),
            P(),
            P("expert", None, "batch"),
            P("expert", "batch", None),
            P("expert", None, "batch"),
            P("expert", "batch", None),
        ),
        out_specs=(
            P(("batch", "expert"), None),
            P("expert", None, "batch"),
            P("expert", "batch", None),
            P("expert", None, "batch"),
            P("expert", "batch", None),
            P(("batch", "expert"), None, None),
        ),
        check_vma=False,
    )
```

```python
import functools

import jax
import jax.numpy as jnp
from jax import lax
from jax.experimental import pallas as pl
from jax.experimental.pallas import tpu as pltpu
from jax.sharding import PartitionSpec as P

SHARED = 64
PRIV = 8
DOMAINS = 8
PRIVATE = 64
GATES = 72
CAP = 4
BF = jnp.bfloat16
F32 = jnp.float32


TURNED = (((0,), (0,)), ((), ()))
TURNED_RIGHT = (((1,), (1,)), ((), ()))


def turn(values, step):
    size = lax.axis_size("batch")
    return lax.ppermute(values, "batch", [(i, (i + step) % size) for i in range(size)])


def near_blocks(pair):
    before_shared = turn(pair[0], 1)
    after_private = turn(pair[1], -1)
    return [before_shared, turn(pair[1], 1), turn(pair[0], -1), after_private]


def far_blocks(near):
    return [turn(near[0], 1), turn(near[3], -1)]


def plus(first, second):
    return (first.astype(F32) + second.astype(F32)).astype(BF)


def scatter_ring(own, near, far):
    before_shared, before_private, after_shared, after_private = near
    via_right = turn(far[0], 1)
    via_left = turn(far[1], -1)
    after_private, before_shared, via_right, via_left = lax.optimization_barrier(
        (after_private, before_shared, via_right, via_left)
    )
    right_private = turn(after_private, 1)
    left_shared = turn(before_shared, -1)
    right_shared = turn(plus(after_shared, via_right), 1)
    left_private = turn(plus(before_private, via_left), -1)
    return by_peer(own[0], right_shared, left_shared, own[1], right_private, left_private)


SPAN = 128


def chosen_rows(kind):
    row = lax.broadcasted_iota(jnp.int32, (SPAN, 2 * SPAN), 0)
    mixed = lax.broadcasted_iota(jnp.int32, (SPAN, 2 * SPAN), 1)
    place = row // CAP * (2 * CAP) + kind * CAP + row % CAP
    return (place == mixed).astype(F32).astype(BF)


def by_kind_kernel(values, *results):
    for kind, result in enumerate(results):
        chosen = chosen_rows(kind)
        for start in range(0, result.shape[0], SPAN):
            result[start : start + SPAN, :] = jnp.dot(
                chosen, values[2 * start : 2 * start + 2 * SPAN, :], preferred_element_type=F32
            ).astype(BF)


def by_kind(values):
    height, features = values.shape
    return list(
        pl.pallas_call(
            by_kind_kernel,
            out_shape=[jax.ShapeDtypeStruct((height // 2, features), BF)] * 2,
            compiler_params=pltpu.CompilerParams(vmem_limit_bytes=16 << 20),
        )(values)
    )


def by_peer_kernel(*refs):
    result = refs[-1]
    for start in range(0, result.shape[0], 2 * SPAN):
        total = 0.0
        for kind in range(2):
            here = slice(start // 2, start // 2 + SPAN)
            parts = [ref[here, :].astype(F32) for ref in refs[3 * kind : 3 * kind + 3]]
            total = total + lax.dot_general(
                chosen_rows(kind),
                (parts[0] + parts[1] + parts[2]).astype(BF),
                TURNED,
                preferred_element_type=F32,
            )
        result[start : start + 2 * SPAN, :] = total.astype(BF)


def by_peer(*parts):
    height, features = parts[0].shape
    return pl.pallas_call(
        by_peer_kernel,
        out_shape=jax.ShapeDtypeStruct((2 * height, features), BF),
        compiler_params=pltpu.CompilerParams(vmem_limit_bytes=16 << 20),
    )(*parts)


def forward_kernel(kinds, *refs):
    blocks = len(kinds)
    rows, weights = refs[:blocks], refs[blocks : blocks + 4]
    pre_out = refs[blocks + 4 : 2 * blocks + 4]
    part_out = refs[2 * blocks + 4 : 3 * blocks + 4]
    rows_held, pre_held, part_held, ins, outs, row_sem, weight_sem, out_sem = refs[3 * blocks + 4 :]
    row_copies = [
        pltpu.make_async_copy(rows[n], rows_held.at[n], row_sem.at[n]) for n in range(blocks)
    ]
    in_copies = [pltpu.make_async_copy(weights[n], ins.at[n], weight_sem.at[n]) for n in range(2)]
    out_copies = [
        pltpu.make_async_copy(weights[2 + n], outs.at[n], weight_sem.at[2 + n]) for n in range(2)
    ]
    for copy in (row_copies[0], in_copies[kinds[0]], out_copies[kinds[0]]):
        copy.start()
    for copy in row_copies[1:]:
        copy.start()
    for copy in (in_copies[1 - kinds[0]], out_copies[1 - kinds[0]]):
        copy.start()
    results = []
    seen = set()
    for n, kind in enumerate(kinds):
        row_copies[n].wait()
        if kind not in seen:
            in_copies[kind].wait()
        pre = jnp.dot(rows_held[n], ins[kind], preferred_element_type=F32)
        pre_held[n] = pre
        results.append(pltpu.make_async_copy(pre_held.at[n], pre_out[n], out_sem.at[2 * n]))
        results[-1].start()
        act = pre * (0.5 * jnp.tanh(0.5 * pre) + 0.5)
        if kind not in seen:
            out_copies[kind].wait()
        seen.add(kind)
        part = jnp.dot(act.astype(BF), outs[kind], preferred_element_type=F32)
        part_held[n] = part.astype(BF)
        results.append(pltpu.make_async_copy(part_held.at[n], part_out[n], out_sem.at[2 * n + 1]))
        results[-1].start()
    for copy in results:
        copy.wait()


def forward(rows, kinds, weights):
    blocks = len(rows)
    features, hidden = weights[0].shape
    height = rows[0].shape[0]
    results = pl.pallas_call(
        functools.partial(forward_kernel, kinds),
        in_specs=[pl.BlockSpec(memory_space=pl.ANY)] * (blocks + 4),
        out_specs=[pl.BlockSpec(memory_space=pl.ANY)] * (2 * blocks),
        out_shape=[jax.ShapeDtypeStruct((height, hidden), F32)] * blocks
        + [jax.ShapeDtypeStruct((height, features), BF)] * blocks,
        scratch_shapes=[
            pltpu.VMEM((blocks, height, features), BF),
            pltpu.VMEM((blocks, height, hidden), F32),
            pltpu.VMEM((blocks, height, features), BF),
            pltpu.VMEM((2, features, hidden), BF),
            pltpu.VMEM((2, hidden, features), BF),
            pltpu.SemaphoreType.DMA((blocks,)),
            pltpu.SemaphoreType.DMA((4,)),
            pltpu.SemaphoreType.DMA((2 * blocks,)),
        ],
        compiler_params=pltpu.CompilerParams(vmem_limit_bytes=60 << 20),
        cost_estimate=pl.CostEstimate(
            flops=4 * blocks * height * features * hidden,
            bytes_accessed=8 * features * hidden + 4 * blocks * height * (features + hidden),
            transcendentals=blocks * height * hidden,
        ),
    )(*rows, *weights)
    return list(results[:blocks]), list(results[blocks:])


def backward_kernel(blocks, *refs):
    total = 2 * blocks
    rows, pres, sent = refs[:total], refs[total : 2 * total], refs[2 * total : 3 * total]
    weights, grads = refs[3 * total : 3 * total + 2], refs[3 * total + 2 : 3 * total + 6]
    rows_held, pre_held, sent_held, outs, acts, backs = refs[3 * total + 6 : 3 * total + 12]
    grads_held = refs[3 * total + 12 : 3 * total + 16]
    source_sem, weight_sem, grad_sem = refs[3 * total + 16 :]
    height = rows[0].shape[0]
    weight_copies = [
        pltpu.make_async_copy(weights[kind], outs.at[kind], weight_sem.at[kind])
        for kind in range(2)
    ]
    copies = []
    for kind in range(2):
        weight_copies[kind].start()
        for n in range(blocks):
            block = kind * blocks + n
            where = pl.ds(n * height, height)
            trio = [
                pltpu.make_async_copy(
                    source[block], held.at[kind, where, :], source_sem.at[3 * block + number]
                )
                for number, (source, held) in enumerate(
                    ((sent, sent_held), (pres, pre_held), (rows, rows_held))
                )
            ]
            for copy in trio:
                copy.start()
            copies.append(trio)
    results = []
    for kind in range(2):
        weight_copies[kind].wait()
        for n in range(blocks):
            for copy in copies[kind * blocks + n]:
                copy.wait()
            here = slice(n * height, (n + 1) * height)
            pre = pre_held[kind, here, :]
            sigmoid = 0.5 * jnp.tanh(0.5 * pre) + 0.5
            slope = sigmoid * (1.0 + pre * (1.0 - sigmoid))
            back = lax.dot_general(
                sent_held[kind, here, :], outs[kind], TURNED_RIGHT, preferred_element_type=F32
            )
            acts[here, :] = (pre * sigmoid).astype(BF)
            backs[here, :] = (back * slope).astype(BF)
        grads_held[2 * kind + 1][...] = lax.dot_general(
            acts[...], sent_held[kind], TURNED, preferred_element_type=F32
        ).astype(BF)
        results.append(
            pltpu.make_async_copy(
                grads_held[2 * kind + 1], grads[2 * kind + 1].at[0], grad_sem.at[2 * kind + 1]
            )
        )
        results[-1].start()
        grads_held[2 * kind][...] = lax.dot_general(
            rows_held[kind], backs[...], TURNED, preferred_element_type=F32
        ).astype(BF)
        results.append(
            pltpu.make_async_copy(grads_held[2 * kind], grads[2 * kind].at[0], grad_sem.at[2 * kind])
        )
        results[-1].start()
    for copy in results:
        copy.wait()


def backward(rows, pres, sent, weight_out_s, weight_out_p):
    hidden, features = weight_out_s.shape
    blocks = len(rows) // 2
    height = blocks * rows[0].shape[0]
    shapes = ((features, hidden), (hidden, features)) * 2
    return pl.pallas_call(
        functools.partial(backward_kernel, blocks),
        in_specs=[pl.BlockSpec(memory_space=pl.ANY)] * (6 * blocks + 2),
        out_specs=[pl.BlockSpec(memory_space=pl.ANY)] * 4,
        out_shape=[jax.ShapeDtypeStruct((1,) + shape, BF) for shape in shapes],
        scratch_shapes=[
            pltpu.VMEM((2, height, features), BF),
            pltpu.VMEM((2, height, hidden), F32),
            pltpu.VMEM((2, height, features), BF),
            pltpu.VMEM((2, hidden, features), BF),
            pltpu.VMEM((height, hidden), BF),
            pltpu.VMEM((height, hidden), BF),
        ]
        + [pltpu.VMEM(shape, BF) for shape in shapes]
        + [
            pltpu.SemaphoreType.DMA((6 * blocks,)),
            pltpu.SemaphoreType.DMA((2,)),
            pltpu.SemaphoreType.DMA((4,)),
        ],
        compiler_params=pltpu.CompilerParams(vmem_limit_bytes=60 << 20),
        cost_estimate=pl.CostEstimate(
            flops=12 * height * features * hidden,
            bytes_accessed=8 * height * (features + hidden) + 12 * features * hidden,
            transcendentals=2 * height * hidden,
        ),
    )(*rows, *pres, *sent, weight_out_s, weight_out_p)


def pack_kernel(domain, shared, private, tokens, target_ref, packed_ref):
    height = tokens.shape[0]
    order = lax.broadcasted_iota(jnp.int32, (height, height), 0)
    ahead = (order < lax.broadcasted_iota(jnp.int32, (height, height), 1)).astype(F32).astype(BF)
    experts = lax.broadcasted_iota(jnp.int32, (SHARED, height), 0)
    cells = lax.broadcasted_iota(jnp.int32, (packed_ref.shape[0], height), 0)
    placed = jnp.zeros(cells.shape, F32)
    for kind in range(2):
        ids = shared[...] if kind == 0 else domain[...] * PRIV + private[...]
        onehot = [(ids[k : k + 1, :] == experts).astype(F32) for k in range(2)]
        both = (onehot[0] + onehot[1]).astype(BF)
        earlier = jnp.dot(both, ahead, preferred_element_type=F32)
        for k in range(2):
            slot = jnp.sum(onehot[k] * earlier, axis=0, keepdims=True).astype(jnp.int32)
            cell = ids[k : k + 1, :] * (2 * CAP) + kind * CAP + slot
            cell = jnp.where(slot < CAP, cell, -1)
            placed = placed + (cell == cells).astype(F32)
            target_ref[2 * kind + k : 2 * kind + k + 1, :] = cell
    packed_ref[...] = jnp.dot(
        placed.astype(BF), tokens[...], preferred_element_type=F32
    ).astype(BF)


def pack(domain_ids, shared_ids, private_ids, tokens):
    height, features = tokens.shape
    return pl.pallas_call(
        pack_kernel,
        out_shape=(
            jax.ShapeDtypeStruct((4, height), jnp.int32),
            jax.ShapeDtypeStruct((SHARED * 2 * CAP, features), BF),
        ),
        compiler_params=pltpu.CompilerParams(vmem_limit_bytes=16 << 20),
    )(domain_ids[None, :], shared_ids.T, private_ids.T, tokens)


def unpack_kernel(target_ref, gates_ref, cot_ref, returned, mixed_ref, dlogit_ref):
    cells = lax.broadcasted_iota(jnp.int32, (cot_ref.shape[0], returned.shape[0]), 1)
    cot = cot_ref[...].astype(F32)
    gates = gates_ref[...]
    mixed = jnp.zeros(cot.shape, F32)
    dgate = []
    for k in range(4):
        chosen = (target_ref[:, k : k + 1] == cells).astype(F32).astype(BF)
        output = jnp.dot(chosen, returned[...], preferred_element_type=F32)
        mixed = mixed + gates[:, k : k + 1] * output
        dgate.append(jnp.sum(cot * output, axis=1, keepdims=True))
    mixed_ref[...] = mixed.astype(BF)
    mean = sum(gates[:, k : k + 1] * dgate[k] for k in range(4))
    lanes = lax.broadcasted_iota(jnp.int32, (cot.shape[0], 128), 1)
    spread = jnp.zeros(lanes.shape, F32)
    for k in range(4):
        spread = jnp.where(lanes == k, gates[:, k : k + 1] * (dgate[k] - mean), spread)
    dlogit_ref[...] = spread.T[:4, :]


def unpack(targets, gates, cotangent, returned):
    return pl.pallas_call(
        unpack_kernel,
        out_shape=(
            jax.ShapeDtypeStruct(cotangent.shape, BF),
            jax.ShapeDtypeStruct(gates.shape[::-1], F32),
        ),
        compiler_params=pltpu.CompilerParams(vmem_limit_bytes=16 << 20),
    )(targets, gates, cotangent, returned)


def gate_kernel(columns, *refs):
    dlogits, tokens, term_ref = refs[:-2], refs[-2], refs[-1]
    height = dlogits[0].shape[1]
    wide = lax.broadcasted_iota(jnp.int32, (term_ref.shape[1], height), 0)
    spreads = []
    for number, dlogit in enumerate(dlogits):
        spread = jnp.zeros(wide.shape, F32)
        for k in range(4):
            column = columns[k : k + 1, number * height : (number + 1) * height]
            spread = spread + jnp.where(column == wide, dlogit[k : k + 1, :], 0.0)
        spreads.append(spread)
    spread = jnp.concatenate(spreads, axis=1)
    total = 0.0
    for _ in range(3):
        piece = spread.astype(BF)
        spread = spread - piece.astype(F32)
        total = total + lax.dot_general(
            tokens[...], piece, TURNED_RIGHT, preferred_element_type=F32
        )
    term_ref[...] = total.astype(BF)


def gate_term(columns, dlogits, tokens, width):
    return pl.pallas_call(
        gate_kernel,
        out_shape=jax.ShapeDtypeStruct((tokens.shape[0], width), BF),
        compiler_params=pltpu.CompilerParams(vmem_limit_bytes=16 << 20),
    )(columns, *dlogits, tokens)


def exchange(values):
    return lax.all_to_all(values, "expert", split_axis=0, concat_axis=0, tiled=True)


def body(
    tokens,
    cotangent,
    domain_ids,
    shared_ids,
    private_ids,
    gate_weight,
    shared_in,
    shared_out,
    private_in,
    private_out,
):
    height, features = tokens.shape
    columns_all = DOMAINS * GATES
    n_batch = lax.axis_size("batch")
    me = lax.axis_index("batch")
    weights = (shared_in[0], private_in[0], shared_out[0], private_out[0])

    targets, packed = pack(domain_ids, shared_ids, private_ids, tokens)
    base = domain_ids[:, None] * GATES
    columns = jnp.concatenate([base + shared_ids, base + SHARED + private_ids], axis=1)
    targets, packed, tokens = lax.optimization_barrier((targets, packed, tokens))
    got = exchange(packed.reshape(-1, 2 * CAP, features))
    cells = jnp.arange(packed.shape[0], dtype=jnp.int32)
    picks = [cells[:, None] == targets[None, k, :] for k in range(4)]
    placed = (picks[0] | picks[1] | picks[2] | picks[3]).astype(BF)

    table = jnp.dot(
        tokens, gate_weight.reshape(features, columns_all), preferred_element_type=F32
    )
    every = jnp.arange(columns_all, dtype=jnp.int32)
    logits = jnp.sum(
        jnp.where(columns[:, :, None] == every[None, None, :], table[:, None, :], 0.0), axis=2
    )
    gates = jax.nn.softmax(logits, axis=1)
    columns, gates = lax.optimization_barrier((columns, gates))
    weight = sum(
        jnp.where(pick, gates[None, :, number], 0.0) for number, pick in enumerate(picks)
    )
    weight = jnp.sum(weight, axis=1, keepdims=True)
    spot = jnp.dot(placed, cotangent, preferred_element_type=F32)
    scaled = (weight * spot).astype(BF)

    width = features // n_batch
    columns_t = columns.T
    column_set = [columns_t]
    token_set = [lax.dynamic_slice_in_dim(tokens, me * width, width, axis=1)]
    for step in range(1, n_batch):
        to = (me + step) % n_batch
        token_set.append(turn(lax.dynamic_slice_in_dim(tokens, to * width, width, axis=1), step))
        column_set.append(turn(columns_t, step))
    token_part = jnp.concatenate(token_set, axis=0).T
    column_part = jnp.concatenate(column_set, axis=1)

    got, scaled, gates, targets, token_part, column_part = lax.optimization_barrier(
        (got, scaled, gates, targets.T, token_part, column_part)
    )

    own = by_kind(got.reshape(-1, features))
    near = near_blocks(own)
    pre_own, part_own = forward(own, (0, 1), weights)
    near[0], near[3], part_own[0] = lax.optimization_barrier((near[0], near[3], part_own[0]))
    far = far_blocks(near)
    pre_first, part_first = forward((near[0], near[3]), (0, 1), weights)
    scaled, part_first[0] = lax.optimization_barrier((scaled, part_first[0]))
    scaled = exchange(scaled.reshape(-1, 2 * CAP, features))
    pre_far, part_far = forward(far, (0, 1), weights)
    pre_second, part_second = forward((near[1], near[2]), (1, 0), weights)
    part_near = (part_first[0], part_second[0], part_second[1], part_first[1])
    pre_near = (pre_first[0], pre_second[0], pre_second[1], pre_first[1])
    summed = scatter_ring(part_own, part_near, part_far)
    summed, scaled = lax.optimization_barrier((summed, scaled))
    returned = exchange(summed.reshape(-1, 2 * CAP, features)).reshape(-1, features)
    sent_own = by_kind(scaled.reshape(-1, features))
    sent_near = near_blocks(sent_own)
    sent_far = far_blocks(sent_near)
    returned, *sent_near = lax.optimization_barrier((returned, *sent_near))

    mixed, dlogit = unpack(targets, gates, cotangent, returned)

    dlogit_set = [dlogit] + [turn(dlogit, step) for step in range(1, n_batch)]
    term = gate_term(column_part, dlogit_set, token_part, columns_all)
    pieces = term.reshape(-1, features // (n_batch * lax.axis_size("expert")), columns_all)
    grad_gate = jnp.sum(exchange(pieces).astype(F32), axis=0).reshape(-1, DOMAINS, GATES)

    ordered = [
        (o[0], n[0], n[2], f[0], o[1], n[1], n[3], f[1])
        for o, n, f in (
            (own, near, far),
            (pre_own, pre_near, pre_far),
            (sent_own, sent_near, sent_far),
        )
    ]
    grads = backward(*ordered, shared_out[0], private_out[0])
    return (mixed, *grads, grad_gate)


def solution(mesh):
    return jax.shard_map(
        body,
        mesh=mesh,
        in_specs=(
            P(("batch", "expert"), None),
            P(("batch", "expert"), None),
            P(("batch", "expert")),
            P(("batch", "expert"), None),
            P(("batch", "expert"), None),
            P(),
            P("expert", None, "batch"),
            P("expert", "batch", None),
            P("expert", None, "batch"),
            P("expert", "batch", None),
        ),
        out_specs=(
            P(("batch", "expert"), None),
            P("expert", None, "batch"),
            P("expert", "batch", None),
            P("expert", None, "batch"),
            P("expert", "batch", None),
            P(("batch", "expert"), None, None),
        ),
        check_vma=False,
    )
```

```python
import functools

import jax
import jax.numpy as jnp
from jax import lax
from jax.experimental import pallas as pl
from jax.experimental.pallas import tpu as pltpu
from jax.sharding import PartitionSpec as P

SHARED = 64
PRIV = 8
DOMAINS = 8
PRIVATE = 64
GATES = 72
CAP = 4
BF = jnp.bfloat16
F32 = jnp.float32


TURNED = (((0,), (0,)), ((), ()))
TURNED_RIGHT = (((1,), (1,)), ((), ()))


def turn(values, step):
    size = lax.axis_size("batch")
    return lax.ppermute(values, "batch", [(i, (i + step) % size) for i in range(size)])


def near_blocks(pair):
    before_shared = turn(pair[0], 1)
    after_private = turn(pair[1], -1)
    return [before_shared, turn(pair[1], 1), turn(pair[0], -1), after_private]


def far_blocks(near):
    return [turn(near[0], 1), turn(near[3], -1)]


def plus(first, second):
    return (first.astype(F32) + second.astype(F32)).astype(BF)


def scatter_ring(own, near, far, behind):
    before_shared, before_private, after_shared, after_private = near
    via_right = turn(far[0], 1)
    via_left = turn(far[1], -1)
    right_private = turn(after_private, 1)
    left_shared = turn(before_shared, -1)
    right_shared = turn(plus(after_shared, via_right), 1)
    left_private = turn(plus(before_private, via_left), -1)
    behind, right_private, left_shared = lax.optimization_barrier(
        (behind, right_private, left_shared)
    )
    return behind, by_peer(own[0], right_shared, left_shared, own[1], right_private, left_private)


SPAN = 128


def chosen_rows(kind):
    row = lax.broadcasted_iota(jnp.int32, (SPAN, 2 * SPAN), 0)
    mixed = lax.broadcasted_iota(jnp.int32, (SPAN, 2 * SPAN), 1)
    place = row // CAP * (2 * CAP) + kind * CAP + row % CAP
    return (place == mixed).astype(F32).astype(BF)


def by_kind_kernel(values, *results):
    for kind, result in enumerate(results):
        chosen = chosen_rows(kind)
        for start in range(0, result.shape[0], SPAN):
            result[start : start + SPAN, :] = jnp.dot(
                chosen, values[2 * start : 2 * start + 2 * SPAN, :], preferred_element_type=F32
            ).astype(BF)


def by_kind(values):
    height, features = values.shape
    return list(
        pl.pallas_call(
            by_kind_kernel,
            out_shape=[jax.ShapeDtypeStruct((height // 2, features), BF)] * 2,
            compiler_params=pltpu.CompilerParams(vmem_limit_bytes=16 << 20),
        )(values)
    )


def by_peer_kernel(*refs):
    result = refs[-1]
    for start in range(0, result.shape[0], 2 * SPAN):
        total = 0.0
        for kind in range(2):
            here = slice(start // 2, start // 2 + SPAN)
            parts = [ref[here, :].astype(F32) for ref in refs[3 * kind : 3 * kind + 3]]
            total = total + lax.dot_general(
                chosen_rows(kind),
                (parts[0] + parts[1] + parts[2]).astype(BF),
                TURNED,
                preferred_element_type=F32,
            )
        result[start : start + 2 * SPAN, :] = total.astype(BF)


def by_peer(*parts):
    height, features = parts[0].shape
    return pl.pallas_call(
        by_peer_kernel,
        out_shape=jax.ShapeDtypeStruct((2 * height, features), BF),
        compiler_params=pltpu.CompilerParams(vmem_limit_bytes=16 << 20),
    )(*parts)


def forward_kernel(kinds, *refs):
    blocks = len(kinds)
    rows, weights = refs[:blocks], refs[blocks : blocks + 4]
    pre_out = refs[blocks + 4 : 2 * blocks + 4]
    part_out = refs[2 * blocks + 4 : 3 * blocks + 4]
    rows_held, pre_held, part_held, ins, outs, row_sem, weight_sem, out_sem = refs[3 * blocks + 4 :]
    row_copies = [
        pltpu.make_async_copy(rows[n], rows_held.at[n], row_sem.at[n]) for n in range(blocks)
    ]
    in_copies = [pltpu.make_async_copy(weights[n], ins.at[n], weight_sem.at[n]) for n in range(2)]
    out_copies = [
        pltpu.make_async_copy(weights[2 + n], outs.at[n], weight_sem.at[2 + n]) for n in range(2)
    ]
    for copy in (row_copies[0], in_copies[kinds[0]], out_copies[kinds[0]]):
        copy.start()
    for copy in row_copies[1:]:
        copy.start()
    for copy in (in_copies[1 - kinds[0]], out_copies[1 - kinds[0]]):
        copy.start()
    results = []
    seen = set()
    for n, kind in enumerate(kinds):
        row_copies[n].wait()
        if kind not in seen:
            in_copies[kind].wait()
        pre = jnp.dot(rows_held[n], ins[kind], preferred_element_type=F32)
        pre_held[n] = pre
        results.append(pltpu.make_async_copy(pre_held.at[n], pre_out[n], out_sem.at[2 * n]))
        results[-1].start()
        act = pre * (0.5 * jnp.tanh(0.5 * pre) + 0.5)
        if kind not in seen:
            out_copies[kind].wait()
        seen.add(kind)
        part = jnp.dot(act.astype(BF), outs[kind], preferred_element_type=F32)
        part_held[n] = part.astype(BF)
        results.append(pltpu.make_async_copy(part_held.at[n], part_out[n], out_sem.at[2 * n + 1]))
        results[-1].start()
    for copy in results:
        copy.wait()


def forward(rows, kinds, weights):
    blocks = len(rows)
    features, hidden = weights[0].shape
    height = rows[0].shape[0]
    results = pl.pallas_call(
        functools.partial(forward_kernel, kinds),
        in_specs=[pl.BlockSpec(memory_space=pl.ANY)] * (blocks + 4),
        out_specs=[pl.BlockSpec(memory_space=pl.ANY)] * (2 * blocks),
        out_shape=[jax.ShapeDtypeStruct((height, hidden), F32)] * blocks
        + [jax.ShapeDtypeStruct((height, features), BF)] * blocks,
        scratch_shapes=[
            pltpu.VMEM((blocks, height, features), BF),
            pltpu.VMEM((blocks, height, hidden), F32),
            pltpu.VMEM((blocks, height, features), BF),
            pltpu.VMEM((2, features, hidden), BF),
            pltpu.VMEM((2, hidden, features), BF),
            pltpu.SemaphoreType.DMA((blocks,)),
            pltpu.SemaphoreType.DMA((4,)),
            pltpu.SemaphoreType.DMA((2 * blocks,)),
        ],
        compiler_params=pltpu.CompilerParams(vmem_limit_bytes=60 << 20),
        cost_estimate=pl.CostEstimate(
            flops=4 * blocks * height * features * hidden,
            bytes_accessed=8 * features * hidden + 4 * blocks * height * (features + hidden),
            transcendentals=blocks * height * hidden,
        ),
    )(*rows, *weights)
    return list(results[:blocks]), list(results[blocks:])


def backward_kernel(blocks, *refs):
    total = 2 * blocks
    rows, pres, sent = refs[:total], refs[total : 2 * total], refs[2 * total : 3 * total]
    weights, grads = refs[3 * total : 3 * total + 2], refs[3 * total + 2 : 3 * total + 6]
    rows_held, pre_held, sent_held, outs, acts, backs = refs[3 * total + 6 : 3 * total + 12]
    grads_held = refs[3 * total + 12 : 3 * total + 16]
    source_sem, weight_sem, grad_sem = refs[3 * total + 16 :]
    height = rows[0].shape[0]
    weight_copies = [
        pltpu.make_async_copy(weights[kind], outs.at[kind], weight_sem.at[kind])
        for kind in range(2)
    ]
    copies = []
    for kind in range(2):
        weight_copies[kind].start()
        for n in range(blocks):
            block = kind * blocks + n
            where = pl.ds(n * height, height)
            trio = [
                pltpu.make_async_copy(
                    source[block], held.at[kind, where, :], source_sem.at[3 * block + number]
                )
                for number, (source, held) in enumerate(
                    ((sent, sent_held), (pres, pre_held), (rows, rows_held))
                )
            ]
            for copy in trio:
                copy.start()
            copies.append(trio)
    results = []
    for kind in range(2):
        weight_copies[kind].wait()
        for n in range(blocks):
            for copy in copies[kind * blocks + n]:
                copy.wait()
            here = slice(n * height, (n + 1) * height)
            pre = pre_held[kind, here, :]
            sigmoid = 0.5 * jnp.tanh(0.5 * pre) + 0.5
            slope = sigmoid * (1.0 + pre * (1.0 - sigmoid))
            back = lax.dot_general(
                sent_held[kind, here, :], outs[kind], TURNED_RIGHT, preferred_element_type=F32
            )
            acts[here, :] = (pre * sigmoid).astype(BF)
            backs[here, :] = (back * slope).astype(BF)
        grads_held[2 * kind + 1][...] = lax.dot_general(
            acts[...], sent_held[kind], TURNED, preferred_element_type=F32
        ).astype(BF)
        results.append(
            pltpu.make_async_copy(
                grads_held[2 * kind + 1], grads[2 * kind + 1].at[0], grad_sem.at[2 * kind + 1]
            )
        )
        results[-1].start()
        grads_held[2 * kind][...] = lax.dot_general(
            rows_held[kind], backs[...], TURNED, preferred_element_type=F32
        ).astype(BF)
        results.append(
            pltpu.make_async_copy(grads_held[2 * kind], grads[2 * kind].at[0], grad_sem.at[2 * kind])
        )
        results[-1].start()
    for copy in results:
        copy.wait()


def backward(rows, pres, sent, weight_out_s, weight_out_p):
    hidden, features = weight_out_s.shape
    blocks = len(rows) // 2
    height = blocks * rows[0].shape[0]
    shapes = ((features, hidden), (hidden, features)) * 2
    return pl.pallas_call(
        functools.partial(backward_kernel, blocks),
        in_specs=[pl.BlockSpec(memory_space=pl.ANY)] * (6 * blocks + 2),
        out_specs=[pl.BlockSpec(memory_space=pl.ANY)] * 4,
        out_shape=[jax.ShapeDtypeStruct((1,) + shape, BF) for shape in shapes],
        scratch_shapes=[
            pltpu.VMEM((2, height, features), BF),
            pltpu.VMEM((2, height, hidden), F32),
            pltpu.VMEM((2, height, features), BF),
            pltpu.VMEM((2, hidden, features), BF),
            pltpu.VMEM((height, hidden), BF),
            pltpu.VMEM((height, hidden), BF),
        ]
        + [pltpu.VMEM(shape, BF) for shape in shapes]
        + [
            pltpu.SemaphoreType.DMA((6 * blocks,)),
            pltpu.SemaphoreType.DMA((2,)),
            pltpu.SemaphoreType.DMA((4,)),
        ],
        compiler_params=pltpu.CompilerParams(vmem_limit_bytes=60 << 20),
        cost_estimate=pl.CostEstimate(
            flops=12 * height * features * hidden,
            bytes_accessed=8 * height * (features + hidden) + 12 * features * hidden,
            transcendentals=2 * height * hidden,
        ),
    )(*rows, *pres, *sent, weight_out_s, weight_out_p)


def pack_kernel(domain, shared, private, tokens, target_ref, packed_ref):
    height = tokens.shape[0]
    order = lax.broadcasted_iota(jnp.int32, (height, height), 0)
    ahead = (order < lax.broadcasted_iota(jnp.int32, (height, height), 1)).astype(F32).astype(BF)
    experts = lax.broadcasted_iota(jnp.int32, (SHARED, height), 0)
    cells = lax.broadcasted_iota(jnp.int32, (packed_ref.shape[0], height), 0)
    placed = jnp.zeros(cells.shape, F32)
    for kind in range(2):
        ids = shared[...] if kind == 0 else domain[...] * PRIV + private[...]
        onehot = [(ids[k : k + 1, :] == experts).astype(F32) for k in range(2)]
        both = (onehot[0] + onehot[1]).astype(BF)
        earlier = jnp.dot(both, ahead, preferred_element_type=F32)
        for k in range(2):
            slot = jnp.sum(onehot[k] * earlier, axis=0, keepdims=True).astype(jnp.int32)
            cell = ids[k : k + 1, :] * (2 * CAP) + kind * CAP + slot
            cell = jnp.where(slot < CAP, cell, -1)
            placed = placed + (cell == cells).astype(F32)
            target_ref[2 * kind + k : 2 * kind + k + 1, :] = cell
    packed_ref[...] = jnp.dot(
        placed.astype(BF), tokens[...], preferred_element_type=F32
    ).astype(BF)


def pack(domain_ids, shared_ids, private_ids, tokens):
    height, features = tokens.shape
    return pl.pallas_call(
        pack_kernel,
        out_shape=(
            jax.ShapeDtypeStruct((4, height), jnp.int32),
            jax.ShapeDtypeStruct((SHARED * 2 * CAP, features), BF),
        ),
    )(domain_ids[None, :], shared_ids.T, private_ids.T, tokens)


def unpack_kernel(target_ref, gates_ref, cot_ref, returned, mixed_ref, dlogit_ref):
    cells = lax.broadcasted_iota(jnp.int32, (cot_ref.shape[0], returned.shape[0]), 1)
    cot = cot_ref[...].astype(F32)
    gates = gates_ref[...]
    mixed = jnp.zeros(cot.shape, F32)
    dgate = []
    for k in range(4):
        chosen = (target_ref[:, k : k + 1] == cells).astype(F32).astype(BF)
        output = jnp.dot(chosen, returned[...], preferred_element_type=F32)
        mixed = mixed + gates[:, k : k + 1] * output
        dgate.append(jnp.sum(cot * output, axis=1, keepdims=True))
    mixed_ref[...] = mixed.astype(BF)
    mean = sum(gates[:, k : k + 1] * dgate[k] for k in range(4))
    lanes = lax.broadcasted_iota(jnp.int32, (cot.shape[0], 128), 1)
    spread = jnp.zeros(lanes.shape, F32)
    for k in range(4):
        spread = jnp.where(lanes == k, gates[:, k : k + 1] * (dgate[k] - mean), spread)
    dlogit_ref[...] = spread.T[:4, :]


def unpack(targets, gates, cotangent, returned):
    return pl.pallas_call(
        unpack_kernel,
        out_shape=(
            jax.ShapeDtypeStruct(cotangent.shape, BF),
            jax.ShapeDtypeStruct(gates.shape[::-1], F32),
        ),
        compiler_params=pltpu.CompilerParams(vmem_limit_bytes=16 << 20),
    )(targets, gates, cotangent, returned)


def gate_kernel(columns, *refs):
    dlogits, tokens, term_ref = refs[:-2], refs[-2], refs[-1]
    height = dlogits[0].shape[1]
    wide = lax.broadcasted_iota(jnp.int32, (term_ref.shape[1], height), 0)
    spreads = []
    for number, dlogit in enumerate(dlogits):
        spread = jnp.zeros(wide.shape, F32)
        for k in range(4):
            column = columns[k : k + 1, number * height : (number + 1) * height]
            spread = spread + jnp.where(column == wide, dlogit[k : k + 1, :], 0.0)
        spreads.append(spread)
    spread = jnp.concatenate(spreads, axis=1)
    total = 0.0
    for _ in range(3):
        piece = spread.astype(BF)
        spread = spread - piece.astype(F32)
        total = total + lax.dot_general(
            tokens[...], piece, TURNED_RIGHT, preferred_element_type=F32
        )
    term_ref[...] = total.astype(BF)


def gate_term(columns, dlogits, tokens, width):
    return pl.pallas_call(
        gate_kernel,
        out_shape=jax.ShapeDtypeStruct((tokens.shape[0], width), BF),
        compiler_params=pltpu.CompilerParams(vmem_limit_bytes=16 << 20),
    )(columns, *dlogits, tokens)


def exchange(values):
    return lax.all_to_all(values, "expert", split_axis=0, concat_axis=0, tiled=True)


def body(
    tokens,
    cotangent,
    domain_ids,
    shared_ids,
    private_ids,
    gate_weight,
    shared_in,
    shared_out,
    private_in,
    private_out,
):
    height, features = tokens.shape
    columns_all = DOMAINS * GATES
    n_batch = lax.axis_size("batch")
    me = lax.axis_index("batch")
    weights = (shared_in[0], private_in[0], shared_out[0], private_out[0])

    targets, packed = pack(domain_ids, shared_ids, private_ids, tokens)
    base = domain_ids[:, None] * GATES
    columns = jnp.concatenate([base + shared_ids, base + SHARED + private_ids], axis=1)
    targets, packed, tokens = lax.optimization_barrier((targets, packed, tokens))
    got = exchange(packed.reshape(-1, 2 * CAP, features))
    cells = jnp.arange(packed.shape[0], dtype=jnp.int32)
    picks = [cells[:, None] == targets[None, k, :] for k in range(4)]
    placed = (picks[0] | picks[1] | picks[2] | picks[3]).astype(BF)

    table = jnp.dot(
        tokens, gate_weight.reshape(features, columns_all), preferred_element_type=F32
    )
    every = jnp.arange(columns_all, dtype=jnp.int32)
    logits = jnp.sum(
        jnp.where(columns[:, :, None] == every[None, None, :], table[:, None, :], 0.0), axis=2
    )
    gates = jax.nn.softmax(logits, axis=1)
    columns, gates = lax.optimization_barrier((columns, gates))
    weight = sum(
        jnp.where(pick, gates[None, :, number], 0.0) for number, pick in enumerate(picks)
    )
    weight = jnp.sum(weight, axis=1, keepdims=True)
    spot = jnp.dot(placed, cotangent, preferred_element_type=F32)
    scaled = (weight * spot).astype(BF)

    width = features // n_batch
    columns_t = columns.T
    column_set = [columns_t]
    token_set = [lax.dynamic_slice_in_dim(tokens, me * width, width, axis=1)]
    for step in range(1, n_batch):
        to = (me + step) % n_batch
        token_set.append(turn(lax.dynamic_slice_in_dim(tokens, to * width, width, axis=1), step))
        column_set.append(turn(columns_t, step))
    token_part = jnp.concatenate(token_set, axis=0).T
    column_part = jnp.concatenate(column_set, axis=1)

    got, scaled, gates, targets, token_part, column_part = lax.optimization_barrier(
        (got, scaled, gates, targets.T, token_part, column_part)
    )

    own = by_kind(got.reshape(-1, features))
    near = near_blocks(own)
    pre_own, part_own = forward(own, (0, 1), weights)
    scaled, part_own[0] = lax.optimization_barrier((scaled, part_own[0]))
    near[0], near[3], part_own[1] = lax.optimization_barrier((near[0], near[3], part_own[1]))
    far = far_blocks(near)
    pre_first, part_first = forward((near[0], near[3]), (0, 1), weights)
    far[0], part_first[0] = lax.optimization_barrier((far[0], part_first[0]))
    scaled = exchange(scaled.reshape(-1, 2 * CAP, features))
    pre_far, part_far = forward(far, (0, 1), weights)
    pre_second, part_second = forward((near[1], near[2]), (1, 0), weights)
    part_near = (part_first[0], part_second[0], part_second[1], part_first[1])
    pre_near = (pre_first[0], pre_second[0], pre_second[1], pre_first[1])
    scaled, summed = scatter_ring(part_own, part_near, part_far, scaled)
    sent_own = by_kind(scaled.reshape(-1, features))
    summed, *sent_own = lax.optimization_barrier((summed, *sent_own))
    sent_near = near_blocks(sent_own)
    returned = exchange(summed.reshape(-1, 2 * CAP, features)).reshape(-1, features)
    sent_far = far_blocks(sent_near)
    returned, *sent_near = lax.optimization_barrier((returned, *sent_near))

    mixed, dlogit = unpack(targets, gates, cotangent, returned)

    dlogit_set = [dlogit] + [turn(dlogit, step) for step in range(1, n_batch)]
    term = gate_term(column_part, dlogit_set, token_part, columns_all)
    pieces = term.reshape(-1, features // (n_batch * lax.axis_size("expert")), columns_all)
    grad_gate = jnp.sum(exchange(pieces).astype(F32), axis=0).reshape(-1, DOMAINS, GATES)

    ordered = [
        (o[0], n[0], n[2], f[0], o[1], n[1], n[3], f[1])
        for o, n, f in (
            (own, near, far),
            (pre_own, pre_near, pre_far),
            (sent_own, sent_near, sent_far),
        )
    ]
    grads = backward(*ordered, shared_out[0], private_out[0])
    return (mixed, *grads, grad_gate)


def solution(mesh):
    return jax.shard_map(
        body,
        mesh=mesh,
        in_specs=(
            P(("batch", "expert"), None),
            P(("batch", "expert"), None),
            P(("batch", "expert")),
            P(("batch", "expert"), None),
            P(("batch", "expert"), None),
            P(),
            P("expert", None, "batch"),
            P("expert", "batch", None),
            P("expert", None, "batch"),
            P("expert", "batch", None),
        ),
        out_specs=(
            P(("batch", "expert"), None),
            P("expert", None, "batch"),
            P("expert", "batch", None),
            P("expert", None, "batch"),
            P("expert", "batch", None),
            P(("batch", "expert"), None, None),
        ),
        check_vma=False,
    )
```

```python
import functools

import jax
import jax.numpy as jnp
from jax import lax
from jax.experimental import pallas as pl
from jax.experimental.pallas import tpu as pltpu
from jax.sharding import PartitionSpec as P

SHARED = 64
PRIV = 8
DOMAINS = 8
PRIVATE = 64
GATES = 72
CAP = 4
BF = jnp.bfloat16
F32 = jnp.float32


TURNED = (((0,), (0,)), ((), ()))
TURNED_RIGHT = (((1,), (1,)), ((), ()))


def turn(values, step):
    size = lax.axis_size("batch")
    return lax.ppermute(values, "batch", [(i, (i + step) % size) for i in range(size)])


def near_blocks(pair):
    before_shared = turn(pair[0], 1)
    after_private = turn(pair[1], -1)
    return [before_shared, turn(pair[1], 1), turn(pair[0], -1), after_private]


def far_blocks(near):
    return [turn(near[0], 1), turn(near[3], -1)]


def plus(first, second):
    return (first.astype(F32) + second.astype(F32)).astype(BF)


def scatter_ring(own, near, far, behind):
    before_shared, before_private, after_shared, after_private = near
    via_right = turn(far[0], 1)
    via_left = turn(far[1], -1)
    right_private = turn(after_private, 1)
    left_shared = turn(before_shared, -1)
    right_shared = turn(plus(after_shared, via_right), 1)
    left_private = turn(plus(before_private, via_left), -1)
    behind, right_private, left_shared = lax.optimization_barrier(
        (behind, right_private, left_shared)
    )
    return behind, by_peer(own[0], right_shared, left_shared, own[1], right_private, left_private)


SPAN = 128


def chosen_rows(kind):
    row = lax.broadcasted_iota(jnp.int32, (SPAN, 2 * SPAN), 0)
    mixed = lax.broadcasted_iota(jnp.int32, (SPAN, 2 * SPAN), 1)
    place = row // CAP * (2 * CAP) + kind * CAP + row % CAP
    return (place == mixed).astype(F32).astype(BF)


def by_kind_kernel(values, *results):
    for kind, result in enumerate(results):
        chosen = chosen_rows(kind)
        for start in range(0, result.shape[0], SPAN):
            result[start : start + SPAN, :] = jnp.dot(
                chosen, values[2 * start : 2 * start + 2 * SPAN, :], preferred_element_type=F32
            ).astype(BF)


def by_kind(values):
    height, features = values.shape
    return list(
        pl.pallas_call(
            by_kind_kernel,
            out_shape=[jax.ShapeDtypeStruct((height // 2, features), BF)] * 2,
            compiler_params=pltpu.CompilerParams(vmem_limit_bytes=16 << 20),
        )(values)
    )


def by_peer_kernel(*refs):
    parts, result, held, done = refs[:6], refs[6], refs[7], refs[8]
    copies = [pltpu.make_async_copy(parts[n], held.at[n], done.at[n]) for n in range(6)]
    for copy in copies:
        copy.start()
    for copy in copies:
        copy.wait()
    for start in range(0, result.shape[0], 2 * SPAN):
        total = 0.0
        for kind in range(2):
            here = slice(start // 2, start // 2 + SPAN)
            rows = [held[3 * kind + n, here, :].astype(F32) for n in range(3)]
            total = total + lax.dot_general(
                chosen_rows(kind),
                (rows[0] + rows[1] + rows[2]).astype(BF),
                TURNED,
                preferred_element_type=F32,
            )
        result[start : start + 2 * SPAN, :] = total.astype(BF)


def by_peer(*parts):
    height, features = parts[0].shape
    return pl.pallas_call(
        by_peer_kernel,
        in_specs=[pl.BlockSpec(memory_space=pl.ANY)] * 6,
        out_specs=pl.BlockSpec(memory_space=pltpu.VMEM),
        out_shape=jax.ShapeDtypeStruct((2 * height, features), BF),
        scratch_shapes=[
            pltpu.VMEM((6, height, features), BF),
            pltpu.SemaphoreType.DMA((6,)),
        ],
        compiler_params=pltpu.CompilerParams(vmem_limit_bytes=60 << 20),
    )(*parts)


def forward_kernel(kinds, *refs):
    blocks = len(kinds)
    rows, weights = refs[:blocks], refs[blocks : blocks + 4]
    pre_out = refs[blocks + 4 : 2 * blocks + 4]
    part_out = refs[2 * blocks + 4 : 3 * blocks + 4]
    rows_held, pre_held, part_held, ins, outs, row_sem, weight_sem, out_sem = refs[3 * blocks + 4 :]
    row_copies = [
        pltpu.make_async_copy(rows[n], rows_held.at[n], row_sem.at[n]) for n in range(blocks)
    ]
    in_copies = [pltpu.make_async_copy(weights[n], ins.at[n], weight_sem.at[n]) for n in range(2)]
    out_copies = [
        pltpu.make_async_copy(weights[2 + n], outs.at[n], weight_sem.at[2 + n]) for n in range(2)
    ]
    for copy in (row_copies[0], in_copies[kinds[0]], out_copies[kinds[0]]):
        copy.start()
    for copy in row_copies[1:]:
        copy.start()
    for copy in (in_copies[1 - kinds[0]], out_copies[1 - kinds[0]]):
        copy.start()
    results = []
    seen = set()
    for n, kind in enumerate(kinds):
        row_copies[n].wait()
        if kind not in seen:
            in_copies[kind].wait()
        pre = jnp.dot(rows_held[n], ins[kind], preferred_element_type=F32)
        pre_held[n] = pre
        results.append(pltpu.make_async_copy(pre_held.at[n], pre_out[n], out_sem.at[2 * n]))
        results[-1].start()
        act = pre * (0.5 * jnp.tanh(0.5 * pre) + 0.5)
        if kind not in seen:
            out_copies[kind].wait()
        seen.add(kind)
        part = jnp.dot(act.astype(BF), outs[kind], preferred_element_type=F32)
        part_held[n] = part.astype(BF)
        results.append(pltpu.make_async_copy(part_held.at[n], part_out[n], out_sem.at[2 * n + 1]))
        results[-1].start()
    for copy in results:
        copy.wait()


def forward(rows, kinds, weights):
    blocks = len(rows)
    features, hidden = weights[0].shape
    height = rows[0].shape[0]
    results = pl.pallas_call(
        functools.partial(forward_kernel, kinds),
        in_specs=[pl.BlockSpec(memory_space=pl.ANY)] * (blocks + 4),
        out_specs=[pl.BlockSpec(memory_space=pl.ANY)] * (2 * blocks),
        out_shape=[jax.ShapeDtypeStruct((height, hidden), F32)] * blocks
        + [jax.ShapeDtypeStruct((height, features), BF)] * blocks,
        scratch_shapes=[
            pltpu.VMEM((blocks, height, features), BF),
            pltpu.VMEM((blocks, height, hidden), F32),
            pltpu.VMEM((blocks, height, features), BF),
            pltpu.VMEM((2, features, hidden), BF),
            pltpu.VMEM((2, hidden, features), BF),
            pltpu.SemaphoreType.DMA((blocks,)),
            pltpu.SemaphoreType.DMA((4,)),
            pltpu.SemaphoreType.DMA((2 * blocks,)),
        ],
        compiler_params=pltpu.CompilerParams(vmem_limit_bytes=60 << 20),
        cost_estimate=pl.CostEstimate(
            flops=4 * blocks * height * features * hidden,
            bytes_accessed=8 * features * hidden + 4 * blocks * height * (features + hidden),
            transcendentals=blocks * height * hidden,
        ),
    )(*rows, *weights)
    return list(results[:blocks]), list(results[blocks:])


def prepare_kernel(blocks, *refs):
    rows, pres = refs[:blocks], refs[blocks : 2 * blocks]
    rows_out, acts_out, slope_out = refs[2 * blocks : 2 * blocks + 3]
    row_held, pre_held, rows_turned, acts_turned, slopes, in_sem, out_sem = refs[2 * blocks + 3 :]
    height = rows[0].shape[0]
    copies = []
    for n in range(blocks):
        copies.append(pltpu.make_async_copy(rows[n], row_held.at[n], in_sem.at[2 * n]))
        copies.append(pltpu.make_async_copy(pres[n], pre_held.at[n], in_sem.at[2 * n + 1]))
    for copy in copies:
        copy.start()
    outs = []
    for n in range(blocks):
        copies[2 * n].wait()
        copies[2 * n + 1].wait()
        kind, place = n // (blocks // 2), n % (blocks // 2)
        where = slice(place * height, (place + 1) * height)
        pre = pre_held[n]
        sigmoid = 0.5 * jnp.tanh(0.5 * pre) + 0.5
        slopes[kind, where, :] = sigmoid * (1.0 + pre * (1.0 - sigmoid))
        acts_turned[kind, :, where] = (pre * sigmoid).astype(BF).T
        rows_turned[kind, :, where] = row_held[n].T
    for number, (held, out) in enumerate(
        ((rows_turned, rows_out), (acts_turned, acts_out), (slopes, slope_out))
    ):
        outs.append(pltpu.make_async_copy(held, out, out_sem.at[number]))
        outs[-1].start()
    for copy in outs:
        copy.wait()


def prepare(rows, pres):
    blocks = len(rows)
    height, features = rows[0].shape
    hidden = pres[0].shape[1]
    total = blocks // 2 * height
    shapes = (((2, features, total), BF), ((2, hidden, total), BF), ((2, total, hidden), F32))
    return pl.pallas_call(
        functools.partial(prepare_kernel, blocks),
        in_specs=[pl.BlockSpec(memory_space=pl.ANY)] * (2 * blocks),
        out_specs=[pl.BlockSpec(memory_space=pl.ANY)] * 3,
        out_shape=[jax.ShapeDtypeStruct(*shape) for shape in shapes],
        scratch_shapes=[
            pltpu.VMEM((blocks, height, features), BF),
            pltpu.VMEM((blocks, height, hidden), F32),
        ]
        + [pltpu.VMEM(*shape) for shape in shapes]
        + [pltpu.SemaphoreType.DMA((2 * blocks,)), pltpu.SemaphoreType.DMA((3,))],
        compiler_params=pltpu.CompilerParams(vmem_limit_bytes=60 << 20),
    )(*rows, *pres)


def backward_kernel(blocks, *refs):
    rows_in, acts_in, slope_in = refs[:3]
    sent = refs[3 : 3 + 2 * blocks]
    weights, grads = refs[3 + 2 * blocks : 5 + 2 * blocks], refs[5 + 2 * blocks : 9 + 2 * blocks]
    rows_turned, acts_turned, slopes, sent_held, outs, backs = refs[9 + 2 * blocks : 15 + 2 * blocks]
    grads_held = refs[15 + 2 * blocks : 19 + 2 * blocks]
    source_sem, sent_sem, weight_sem, grad_sem = refs[19 + 2 * blocks :]
    height = sent[0].shape[0]
    ready = []
    for kind in range(2):
        copies = [pltpu.make_async_copy(weights[kind], outs.at[kind], weight_sem.at[kind])]
        for n in range(blocks):
            block = kind * blocks + n
            copies.append(
                pltpu.make_async_copy(
                    sent[block],
                    sent_held.at[kind, pl.ds(n * height, height), :],
                    sent_sem.at[block],
                )
            )
        for number, (source, held) in enumerate(
            ((acts_in, acts_turned), (slope_in, slopes), (rows_in, rows_turned))
        ):
            copies.append(
                pltpu.make_async_copy(
                    source.at[kind], held.at[kind], source_sem.at[3 * kind + number]
                )
            )
        for copy in copies:
            copy.start()
        ready.append(copies)
    results = []
    for kind in range(2):
        for copy in ready[kind][: blocks + 2]:
            copy.wait()
        grads_held[2 * kind + 1][...] = jnp.dot(
            acts_turned[kind], sent_held[kind], preferred_element_type=F32
        ).astype(BF)
        results.append(
            pltpu.make_async_copy(
                grads_held[2 * kind + 1], grads[2 * kind + 1].at[0], grad_sem.at[2 * kind + 1]
            )
        )
        results[-1].start()
        back = lax.dot_general(
            sent_held[kind], outs[kind], TURNED_RIGHT, preferred_element_type=F32
        )
        for copy in ready[kind][blocks + 2 :]:
            copy.wait()
        backs[...] = (back * slopes[kind]).astype(BF)
        grads_held[2 * kind][...] = jnp.dot(
            rows_turned[kind], backs[...], preferred_element_type=F32
        ).astype(BF)
        results.append(
            pltpu.make_async_copy(grads_held[2 * kind], grads[2 * kind].at[0], grad_sem.at[2 * kind])
        )
        results[-1].start()
    for copy in results:
        copy.wait()


def backward(prepared, sent, weight_out_s, weight_out_p):
    hidden, features = weight_out_s.shape
    blocks = len(sent) // 2
    height = blocks * sent[0].shape[0]
    shapes = ((features, hidden), (hidden, features)) * 2
    return pl.pallas_call(
        functools.partial(backward_kernel, blocks),
        in_specs=[pl.BlockSpec(memory_space=pl.ANY)] * (2 * blocks + 5),
        out_specs=[pl.BlockSpec(memory_space=pl.ANY)] * 4,
        out_shape=[jax.ShapeDtypeStruct((1,) + shape, BF) for shape in shapes],
        scratch_shapes=[
            pltpu.VMEM((2, features, height), BF),
            pltpu.VMEM((2, hidden, height), BF),
            pltpu.VMEM((2, height, hidden), F32),
            pltpu.VMEM((2, height, features), BF),
            pltpu.VMEM((2, hidden, features), BF),
            pltpu.VMEM((height, hidden), BF),
        ]
        + [pltpu.VMEM(shape, BF) for shape in shapes]
        + [
            pltpu.SemaphoreType.DMA((6,)),
            pltpu.SemaphoreType.DMA((2 * blocks,)),
            pltpu.SemaphoreType.DMA((2,)),
            pltpu.SemaphoreType.DMA((4,)),
        ],
        compiler_params=pltpu.CompilerParams(vmem_limit_bytes=60 << 20),
        cost_estimate=pl.CostEstimate(
            flops=12 * height * features * hidden,
            bytes_accessed=8 * height * (features + hidden) + 12 * features * hidden,
            transcendentals=0,
        ),
    )(*prepared, *sent, weight_out_s, weight_out_p)


def pack_kernel(domain, shared, private, tokens, target_ref, packed_ref):
    height = tokens.shape[0]
    order = lax.broadcasted_iota(jnp.int32, (height, height), 0)
    ahead = (order < lax.broadcasted_iota(jnp.int32, (height, height), 1)).astype(F32).astype(BF)
    experts = lax.broadcasted_iota(jnp.int32, (SHARED, height), 0)
    cells = lax.broadcasted_iota(jnp.int32, (packed_ref.shape[0], height), 0)
    placed = jnp.zeros(cells.shape, F32)
    for kind in range(2):
        ids = shared[...] if kind == 0 else domain[...] * PRIV + private[...]
        onehot = [(ids[k : k + 1, :] == experts).astype(F32) for k in range(2)]
        both = (onehot[0] + onehot[1]).astype(BF)
        earlier = jnp.dot(both, ahead, preferred_element_type=F32)
        for k in range(2):
            slot = jnp.sum(onehot[k] * earlier, axis=0, keepdims=True).astype(jnp.int32)
            cell = ids[k : k + 1, :] * (2 * CAP) + kind * CAP + slot
            cell = jnp.where(slot < CAP, cell, -1)
            placed = placed + (cell == cells).astype(F32)
            target_ref[2 * kind + k : 2 * kind + k + 1, :] = cell
    packed_ref[...] = jnp.dot(
        placed.astype(BF), tokens[...], preferred_element_type=F32
    ).astype(BF)


def pack(domain_ids, shared_ids, private_ids, tokens):
    height, features = tokens.shape
    return pl.pallas_call(
        pack_kernel,
        out_shape=(
            jax.ShapeDtypeStruct((4, height), jnp.int32),
            jax.ShapeDtypeStruct((SHARED * 2 * CAP, features), BF),
        ),
    )(domain_ids[None, :], shared_ids.T, private_ids.T, tokens)


def unpack_kernel(target_ref, gates_ref, cot_ref, returned, mixed_ref, dlogit_ref):
    cells = lax.broadcasted_iota(jnp.int32, (cot_ref.shape[0], returned.shape[0]), 1)
    cot = cot_ref[...].astype(F32)
    gates = gates_ref[...]
    mixed = jnp.zeros(cot.shape, F32)
    dgate = []
    for k in range(4):
        chosen = (target_ref[:, k : k + 1] == cells).astype(F32).astype(BF)
        output = jnp.dot(chosen, returned[...], preferred_element_type=F32)
        mixed = mixed + gates[:, k : k + 1] * output
        dgate.append(jnp.sum(cot * output, axis=1, keepdims=True))
    mixed_ref[...] = mixed.astype(BF)
    mean = sum(gates[:, k : k + 1] * dgate[k] for k in range(4))
    lanes = lax.broadcasted_iota(jnp.int32, (cot.shape[0], 128), 1)
    spread = jnp.zeros(lanes.shape, F32)
    for k in range(4):
        spread = jnp.where(lanes == k, gates[:, k : k + 1] * (dgate[k] - mean), spread)
    dlogit_ref[...] = spread.T[:4, :]


def unpack(targets, gates, cotangent, returned):
    return pl.pallas_call(
        unpack_kernel,
        out_shape=(
            jax.ShapeDtypeStruct(cotangent.shape, BF),
            jax.ShapeDtypeStruct(gates.shape[::-1], F32),
        ),
        compiler_params=pltpu.CompilerParams(vmem_limit_bytes=16 << 20),
    )(targets, gates, cotangent, returned)


def gate_kernel(columns, *refs):
    dlogits, tokens, term_ref = refs[:-2], refs[-2], refs[-1]
    height = dlogits[0].shape[1]
    wide = lax.broadcasted_iota(jnp.int32, (term_ref.shape[1], height), 0)
    spreads = []
    for number, dlogit in enumerate(dlogits):
        spread = jnp.zeros(wide.shape, F32)
        for k in range(4):
            column = columns[k : k + 1, number * height : (number + 1) * height]
            spread = spread + jnp.where(column == wide, dlogit[k : k + 1, :], 0.0)
        spreads.append(spread)
    spread = jnp.concatenate(spreads, axis=1)
    total = 0.0
    for _ in range(3):
        piece = spread.astype(BF)
        spread = spread - piece.astype(F32)
        total = total + lax.dot_general(
            tokens[...], piece, TURNED_RIGHT, preferred_element_type=F32
        )
    term_ref[...] = total.astype(BF)


def gate_term(columns, dlogits, tokens, width):
    return pl.pallas_call(
        gate_kernel,
        out_shape=jax.ShapeDtypeStruct((tokens.shape[0], width), BF),
        compiler_params=pltpu.CompilerParams(vmem_limit_bytes=16 << 20),
    )(columns, *dlogits, tokens)


def exchange(values):
    return lax.all_to_all(values, "expert", split_axis=0, concat_axis=0, tiled=True)


def body(
    tokens,
    cotangent,
    domain_ids,
    shared_ids,
    private_ids,
    gate_weight,
    shared_in,
    shared_out,
    private_in,
    private_out,
):
    height, features = tokens.shape
    columns_all = DOMAINS * GATES
    n_batch = lax.axis_size("batch")
    me = lax.axis_index("batch")
    weights = (shared_in[0], private_in[0], shared_out[0], private_out[0])

    targets, packed = pack(domain_ids, shared_ids, private_ids, tokens)
    base = domain_ids[:, None] * GATES
    columns = jnp.concatenate([base + shared_ids, base + SHARED + private_ids], axis=1)
    targets, packed, tokens = lax.optimization_barrier((targets, packed, tokens))
    got = exchange(packed.reshape(-1, 2 * CAP, features))
    cells = jnp.arange(packed.shape[0], dtype=jnp.int32)
    picks = [cells[:, None] == targets[None, k, :] for k in range(4)]
    placed = (picks[0] | picks[1] | picks[2] | picks[3]).astype(BF)

    table = jnp.dot(
        tokens, gate_weight.reshape(features, columns_all), preferred_element_type=F32
    )
    every = jnp.arange(columns_all, dtype=jnp.int32)
    logits = jnp.sum(
        jnp.where(columns[:, :, None] == every[None, None, :], table[:, None, :], 0.0), axis=2
    )
    gates = jax.nn.softmax(logits, axis=1)
    columns, gates = lax.optimization_barrier((columns, gates))
    weight = sum(
        jnp.where(pick, gates[None, :, number], 0.0) for number, pick in enumerate(picks)
    )
    weight = jnp.sum(weight, axis=1, keepdims=True)
    spot = jnp.dot(placed, cotangent, preferred_element_type=F32)
    scaled = (weight * spot).astype(BF)

    width = features // n_batch
    columns_t = columns.T
    column_set = [columns_t]
    token_set = [lax.dynamic_slice_in_dim(tokens, me * width, width, axis=1)]
    for step in range(1, n_batch):
        to = (me + step) % n_batch
        token_set.append(turn(lax.dynamic_slice_in_dim(tokens, to * width, width, axis=1), step))
        column_set.append(turn(columns_t, step))
    token_part = jnp.concatenate(token_set, axis=0).T
    column_part = jnp.concatenate(column_set, axis=1)

    got, scaled, gates, targets, token_part, column_part = lax.optimization_barrier(
        (got, scaled, gates, targets.T, token_part, column_part)
    )

    own = by_kind(got.reshape(-1, features))
    near = near_blocks(own)
    pre_own, part_own = forward(own, (0, 1), weights)
    scaled, part_own[0] = lax.optimization_barrier((scaled, part_own[0]))
    near[0], near[3], part_own[1] = lax.optimization_barrier((near[0], near[3], part_own[1]))
    far = far_blocks(near)
    pre_first, part_first = forward((near[0], near[3]), (0, 1), weights)
    far[0], part_first[0] = lax.optimization_barrier((far[0], part_first[0]))
    scaled = exchange(scaled.reshape(-1, 2 * CAP, features))
    pre_far, part_far = forward(far, (0, 1), weights)
    pre_second, part_second = forward((near[1], near[2]), (1, 0), weights)
    part_near = (part_first[0], part_second[0], part_second[1], part_first[1])
    pre_near = (pre_first[0], pre_second[0], pre_second[1], pre_first[1])
    scaled, summed = scatter_ring(part_own, part_near, part_far, scaled)
    sent_own = by_kind(scaled.reshape(-1, features))
    ordered = [
        (o[0], n[0], n[2], f[0], o[1], n[1], n[3], f[1])
        for o, n, f in ((own, near, far), (pre_own, pre_near, pre_far))
    ]
    summed, sent_own, ordered = lax.optimization_barrier((summed, sent_own, ordered))
    sent_near = near_blocks(sent_own)
    returned = exchange(summed.reshape(-1, 2 * CAP, features)).reshape(-1, features)
    prepared = prepare(*ordered)
    prepared, sent_near[0] = lax.optimization_barrier((prepared, sent_near[0]))
    sent_far = far_blocks(sent_near)
    returned, sent_near = lax.optimization_barrier((returned, sent_near))

    mixed, dlogit = unpack(targets, gates, cotangent, returned)

    dlogit_set = [dlogit] + [turn(dlogit, step) for step in range(1, n_batch)]
    term = gate_term(column_part, dlogit_set, token_part, columns_all)
    pieces = term.reshape(-1, features // (n_batch * lax.axis_size("expert")), columns_all)
    grad_gate = jnp.sum(exchange(pieces).astype(F32), axis=0).reshape(-1, DOMAINS, GATES)

    o, n, f = sent_own, sent_near, sent_far
    sent = (o[0], n[0], n[2], f[0], o[1], n[1], n[3], f[1])
    grads = backward(prepared, sent, shared_out[0], private_out[0])
    return (mixed, *grads, grad_gate)


def solution(mesh):
    return jax.shard_map(
        body,
        mesh=mesh,
        in_specs=(
            P(("batch", "expert"), None),
            P(("batch", "expert"), None),
            P(("batch", "expert")),
            P(("batch", "expert"), None),
            P(("batch", "expert"), None),
            P(),
            P("expert", None, "batch"),
            P("expert", "batch", None),
            P("expert", None, "batch"),
            P("expert", "batch", None),
        ),
        out_specs=(
            P(("batch", "expert"), None),
            P("expert", None, "batch"),
            P("expert", "batch", None),
            P("expert", None, "batch"),
            P("expert", "batch", None),
            P(("batch", "expert"), None, None),
        ),
        check_vma=False,
    )
```

```python
import functools

import jax
import jax.numpy as jnp
from jax import lax
from jax.experimental import pallas as pl
from jax.experimental.pallas import tpu as pltpu
from jax.sharding import PartitionSpec as P

SHARED = 64
PRIV = 8
DOMAINS = 8
PRIVATE = 64
GATES = 72
CAP = 4
BF = jnp.bfloat16
F32 = jnp.float32


TURNED = (((0,), (0,)), ((), ()))
TURNED_RIGHT = (((1,), (1,)), ((), ()))


def turn(values, step):
    size = lax.axis_size("batch")
    return lax.ppermute(values, "batch", [(i, (i + step) % size) for i in range(size)])


def near_blocks(pair):
    before_shared = turn(pair[0], 1)
    after_private = turn(pair[1], -1)
    return [before_shared, turn(pair[1], 1), turn(pair[0], -1), after_private]


def far_blocks(near):
    return [turn(near[0], 1), turn(near[3], -1)]


def plus(first, second):
    return (first.astype(F32) + second.astype(F32)).astype(BF)


def scatter_ring(own, near, far, behind):
    before_shared, before_private, after_shared, after_private = near
    via_right = turn(far[0], 1)
    via_left = turn(far[1], -1)
    right_private = turn(after_private, 1)
    left_shared = turn(before_shared, -1)
    right_shared = turn(plus(after_shared, via_right), 1)
    left_private = turn(plus(before_private, via_left), -1)
    behind, right_private, left_shared = lax.optimization_barrier(
        (behind, right_private, left_shared)
    )
    return behind, by_peer(own[0], right_shared, left_shared, own[1], right_private, left_private)


SPAN = 128


def chosen_rows(kind):
    row = lax.broadcasted_iota(jnp.int32, (SPAN, 2 * SPAN), 0)
    mixed = lax.broadcasted_iota(jnp.int32, (SPAN, 2 * SPAN), 1)
    place = row // CAP * (2 * CAP) + kind * CAP + row % CAP
    return (place == mixed).astype(F32).astype(BF)


def by_kind_kernel(values, *results):
    for kind, result in enumerate(results):
        chosen = chosen_rows(kind)
        for start in range(0, result.shape[0], SPAN):
            result[start : start + SPAN, :] = jnp.dot(
                chosen, values[2 * start : 2 * start + 2 * SPAN, :], preferred_element_type=F32
            ).astype(BF)


def by_kind(values):
    height, features = values.shape
    return list(
        pl.pallas_call(
            by_kind_kernel,
            out_shape=[jax.ShapeDtypeStruct((height // 2, features), BF)] * 2,
            compiler_params=pltpu.CompilerParams(vmem_limit_bytes=16 << 20),
        )(values)
    )


def by_peer_kernel(*refs):
    parts, result, held, done = refs[:6], refs[6], refs[7], refs[8]
    copies = [pltpu.make_async_copy(parts[n], held.at[n], done.at[n]) for n in range(6)]
    for copy in copies:
        copy.start()
    for copy in copies:
        copy.wait()
    for start in range(0, result.shape[0], 2 * SPAN):
        total = 0.0
        for kind in range(2):
            here = slice(start // 2, start // 2 + SPAN)
            rows = [held[3 * kind + n, here, :].astype(F32) for n in range(3)]
            total = total + lax.dot_general(
                chosen_rows(kind),
                (rows[0] + rows[1] + rows[2]).astype(BF),
                TURNED,
                preferred_element_type=F32,
            )
        result[start : start + 2 * SPAN, :] = total.astype(BF)


def by_peer(*parts):
    height, features = parts[0].shape
    return pl.pallas_call(
        by_peer_kernel,
        in_specs=[pl.BlockSpec(memory_space=pl.ANY)] * 6,
        out_specs=pl.BlockSpec(memory_space=pltpu.VMEM),
        out_shape=jax.ShapeDtypeStruct((2 * height, features), BF),
        scratch_shapes=[
            pltpu.VMEM((6, height, features), BF),
            pltpu.SemaphoreType.DMA((6,)),
        ],
        compiler_params=pltpu.CompilerParams(vmem_limit_bytes=60 << 20),
    )(*parts)


def forward_kernel(kinds, *refs):
    blocks = len(kinds)
    rows, weights = refs[:blocks], refs[blocks : blocks + 4]
    pre_out = refs[blocks + 4 : 2 * blocks + 4]
    part_out = refs[2 * blocks + 4 : 3 * blocks + 4]
    rows_held, pre_held, part_held, ins, outs, row_sem, weight_sem, out_sem = refs[3 * blocks + 4 :]
    row_copies = [
        pltpu.make_async_copy(rows[n], rows_held.at[n], row_sem.at[n]) for n in range(blocks)
    ]
    in_copies = [pltpu.make_async_copy(weights[n], ins.at[n], weight_sem.at[n]) for n in range(2)]
    out_copies = [
        pltpu.make_async_copy(weights[2 + n], outs.at[n], weight_sem.at[2 + n]) for n in range(2)
    ]
    for copy in (row_copies[0], in_copies[kinds[0]], out_copies[kinds[0]]):
        copy.start()
    for copy in row_copies[1:]:
        copy.start()
    for copy in (in_copies[1 - kinds[0]], out_copies[1 - kinds[0]]):
        copy.start()
    results = []
    seen = set()
    for n, kind in enumerate(kinds):
        row_copies[n].wait()
        if kind not in seen:
            in_copies[kind].wait()
        pre = jnp.dot(rows_held[n], ins[kind], preferred_element_type=F32)
        pre_held[n] = pre
        results.append(pltpu.make_async_copy(pre_held.at[n], pre_out[n], out_sem.at[2 * n]))
        results[-1].start()
        act = pre * (0.5 * jnp.tanh(0.5 * pre) + 0.5)
        if kind not in seen:
            out_copies[kind].wait()
        seen.add(kind)
        part = jnp.dot(act.astype(BF), outs[kind], preferred_element_type=F32)
        part_held[n] = part.astype(BF)
        results.append(pltpu.make_async_copy(part_held.at[n], part_out[n], out_sem.at[2 * n + 1]))
        results[-1].start()
    for copy in results:
        copy.wait()


def forward(rows, kinds, weights):
    blocks = len(rows)
    features, hidden = weights[0].shape
    height = rows[0].shape[0]
    results = pl.pallas_call(
        functools.partial(forward_kernel, kinds),
        in_specs=[pl.BlockSpec(memory_space=pl.ANY)] * (blocks + 4),
        out_specs=[pl.BlockSpec(memory_space=pl.ANY)] * (2 * blocks),
        out_shape=[jax.ShapeDtypeStruct((height, hidden), F32)] * blocks
        + [jax.ShapeDtypeStruct((height, features), BF)] * blocks,
        scratch_shapes=[
            pltpu.VMEM((blocks, height, features), BF),
            pltpu.VMEM((blocks, height, hidden), F32),
            pltpu.VMEM((blocks, height, features), BF),
            pltpu.VMEM((2, features, hidden), BF),
            pltpu.VMEM((2, hidden, features), BF),
            pltpu.SemaphoreType.DMA((blocks,)),
            pltpu.SemaphoreType.DMA((4,)),
            pltpu.SemaphoreType.DMA((2 * blocks,)),
        ],
        compiler_params=pltpu.CompilerParams(vmem_limit_bytes=60 << 20),
        cost_estimate=pl.CostEstimate(
            flops=4 * blocks * height * features * hidden,
            bytes_accessed=8 * features * hidden + 4 * blocks * height * (features + hidden),
            transcendentals=blocks * height * hidden,
        ),
    )(*rows, *weights)
    return list(results[:blocks]), list(results[blocks:])


def prepare_kernel(blocks, *refs):
    rows, pres = refs[:blocks], refs[blocks : 2 * blocks]
    rows_out, acts_out, slope_out = refs[2 * blocks : 2 * blocks + 3]
    row_held, pre_held, rows_turned, acts_turned, slopes, in_sem, out_sem = refs[2 * blocks + 3 :]
    height = rows[0].shape[0]
    copies = []
    for n in range(blocks):
        copies.append(pltpu.make_async_copy(rows[n], row_held.at[n], in_sem.at[2 * n]))
        copies.append(pltpu.make_async_copy(pres[n], pre_held.at[n], in_sem.at[2 * n + 1]))
    for copy in copies:
        copy.start()
    outs = []
    for n in range(blocks):
        copies[2 * n].wait()
        copies[2 * n + 1].wait()
        kind, place = n // (blocks // 2), n % (blocks // 2)
        where = slice(place * height, (place + 1) * height)
        pre = pre_held[n]
        sigmoid = 0.5 * jnp.tanh(0.5 * pre) + 0.5
        slopes[kind, where, :] = sigmoid * (1.0 + pre * (1.0 - sigmoid))
        acts_turned[kind, :, where] = (pre * sigmoid).astype(BF).T
        rows_turned[kind, :, where] = row_held[n].T
    for number, (held, out) in enumerate(
        ((rows_turned, rows_out), (acts_turned, acts_out), (slopes, slope_out))
    ):
        outs.append(pltpu.make_async_copy(held, out, out_sem.at[number]))
        outs[-1].start()
    for copy in outs:
        copy.wait()


def prepare(rows, pres):
    blocks = len(rows)
    height, features = rows[0].shape
    hidden = pres[0].shape[1]
    total = blocks // 2 * height
    shapes = (((2, features, total), BF), ((2, hidden, total), BF), ((2, total, hidden), F32))
    return pl.pallas_call(
        functools.partial(prepare_kernel, blocks),
        in_specs=[pl.BlockSpec(memory_space=pl.ANY)] * (2 * blocks),
        out_specs=[pl.BlockSpec(memory_space=pl.ANY)] * 3,
        out_shape=[jax.ShapeDtypeStruct(*shape) for shape in shapes],
        scratch_shapes=[
            pltpu.VMEM((blocks, height, features), BF),
            pltpu.VMEM((blocks, height, hidden), F32),
        ]
        + [pltpu.VMEM(*shape) for shape in shapes]
        + [pltpu.SemaphoreType.DMA((2 * blocks,)), pltpu.SemaphoreType.DMA((3,))],
        compiler_params=pltpu.CompilerParams(vmem_limit_bytes=60 << 20),
    )(*rows, *pres)


def backward_kernel(blocks, *refs):
    rows_in, acts_in, slope_in = refs[:3]
    sent = refs[3 : 3 + 2 * blocks]
    weights, grads = refs[3 + 2 * blocks : 5 + 2 * blocks], refs[5 + 2 * blocks : 9 + 2 * blocks]
    rows_turned, acts_turned, slopes, sent_held, outs, backs = refs[9 + 2 * blocks : 15 + 2 * blocks]
    grads_held = refs[15 + 2 * blocks : 19 + 2 * blocks]
    source_sem, sent_sem, weight_sem, grad_sem = refs[19 + 2 * blocks :]
    height = sent[0].shape[0]
    ready = []
    for kind in range(2):
        copies = [pltpu.make_async_copy(weights[kind], outs.at[kind], weight_sem.at[kind])]
        for n in range(blocks):
            block = kind * blocks + n
            copies.append(
                pltpu.make_async_copy(
                    sent[block],
                    sent_held.at[kind, pl.ds(n * height, height), :],
                    sent_sem.at[block],
                )
            )
        for number, (source, held) in enumerate(
            ((acts_in, acts_turned), (slope_in, slopes), (rows_in, rows_turned))
        ):
            copies.append(
                pltpu.make_async_copy(
                    source.at[kind], held.at[kind], source_sem.at[3 * kind + number]
                )
            )
        for copy in copies:
            copy.start()
        ready.append(copies)
    results = []
    for kind in range(2):
        for copy in ready[kind][: blocks + 2]:
            copy.wait()
        grads_held[2 * kind + 1][...] = jnp.dot(
            acts_turned[kind], sent_held[kind], preferred_element_type=F32
        ).astype(BF)
        results.append(
            pltpu.make_async_copy(
                grads_held[2 * kind + 1], grads[2 * kind + 1].at[0], grad_sem.at[2 * kind + 1]
            )
        )
        results[-1].start()
        back = lax.dot_general(
            sent_held[kind], outs[kind], TURNED_RIGHT, preferred_element_type=F32
        )
        for copy in ready[kind][blocks + 2 :]:
            copy.wait()
        backs[...] = (back * slopes[kind]).astype(BF)
        grads_held[2 * kind][...] = jnp.dot(
            rows_turned[kind], backs[...], preferred_element_type=F32
        ).astype(BF)
        results.append(
            pltpu.make_async_copy(grads_held[2 * kind], grads[2 * kind].at[0], grad_sem.at[2 * kind])
        )
        results[-1].start()
    for copy in results:
        copy.wait()


def backward(prepared, sent, weight_out_s, weight_out_p):
    hidden, features = weight_out_s.shape
    blocks = len(sent) // 2
    height = blocks * sent[0].shape[0]
    shapes = ((features, hidden), (hidden, features)) * 2
    return pl.pallas_call(
        functools.partial(backward_kernel, blocks),
        in_specs=[pl.BlockSpec(memory_space=pl.ANY)] * (2 * blocks + 5),
        out_specs=[pl.BlockSpec(memory_space=pl.ANY)] * 4,
        out_shape=[jax.ShapeDtypeStruct((1,) + shape, BF) for shape in shapes],
        scratch_shapes=[
            pltpu.VMEM((2, features, height), BF),
            pltpu.VMEM((2, hidden, height), BF),
            pltpu.VMEM((2, height, hidden), F32),
            pltpu.VMEM((2, height, features), BF),
            pltpu.VMEM((2, hidden, features), BF),
            pltpu.VMEM((height, hidden), BF),
        ]
        + [pltpu.VMEM(shape, BF) for shape in shapes]
        + [
            pltpu.SemaphoreType.DMA((6,)),
            pltpu.SemaphoreType.DMA((2 * blocks,)),
            pltpu.SemaphoreType.DMA((2,)),
            pltpu.SemaphoreType.DMA((4,)),
        ],
        compiler_params=pltpu.CompilerParams(vmem_limit_bytes=60 << 20),
        cost_estimate=pl.CostEstimate(
            flops=12 * height * features * hidden,
            bytes_accessed=8 * height * (features + hidden) + 12 * features * hidden,
            transcendentals=0,
        ),
    )(*prepared, *sent, weight_out_s, weight_out_p)


def pack_kernel(domain, shared, private, tokens, target_ref, packed_ref):
    height = tokens.shape[0]
    order = lax.broadcasted_iota(jnp.int32, (height, height), 0)
    ahead = (order < lax.broadcasted_iota(jnp.int32, (height, height), 1)).astype(F32).astype(BF)
    experts = lax.broadcasted_iota(jnp.int32, (SHARED, height), 0)
    cells = lax.broadcasted_iota(jnp.int32, (packed_ref.shape[0], height), 0)
    placed = jnp.zeros(cells.shape, F32)
    for kind in range(2):
        ids = shared[...] if kind == 0 else domain[...] * PRIV + private[...]
        onehot = [(ids[k : k + 1, :] == experts).astype(F32) for k in range(2)]
        both = (onehot[0] + onehot[1]).astype(BF)
        earlier = jnp.dot(both, ahead, preferred_element_type=F32)
        for k in range(2):
            slot = jnp.sum(onehot[k] * earlier, axis=0, keepdims=True).astype(jnp.int32)
            cell = ids[k : k + 1, :] * (2 * CAP) + kind * CAP + slot
            cell = jnp.where(slot < CAP, cell, -1)
            placed = placed + (cell == cells).astype(F32)
            target_ref[2 * kind + k : 2 * kind + k + 1, :] = cell
    packed_ref[...] = jnp.dot(
        placed.astype(BF), tokens[...], preferred_element_type=F32
    ).astype(BF)


def pack(domain_ids, shared_ids, private_ids, tokens):
    height, features = tokens.shape
    return pl.pallas_call(
        pack_kernel,
        out_shape=(
            jax.ShapeDtypeStruct((4, height), jnp.int32),
            jax.ShapeDtypeStruct((SHARED * 2 * CAP, features), BF),
        ),
    )(domain_ids[None, :], shared_ids.T, private_ids.T, tokens)


def unpack_kernel(target_ref, gates_ref, cot_ref, returned, mixed_ref, dlogit_ref):
    cells = lax.broadcasted_iota(jnp.int32, (cot_ref.shape[0], returned.shape[0]), 1)
    cot = cot_ref[...].astype(F32)
    gates = gates_ref[...]
    mixed = jnp.zeros(cot.shape, F32)
    dgate = []
    for k in range(4):
        chosen = (target_ref[:, k : k + 1] == cells).astype(F32).astype(BF)
        output = jnp.dot(chosen, returned[...], preferred_element_type=F32)
        mixed = mixed + gates[:, k : k + 1] * output
        dgate.append(jnp.sum(cot * output, axis=1, keepdims=True))
    mixed_ref[...] = mixed.astype(BF)
    mean = sum(gates[:, k : k + 1] * dgate[k] for k in range(4))
    lanes = lax.broadcasted_iota(jnp.int32, (cot.shape[0], 128), 1)
    spread = jnp.zeros(lanes.shape, F32)
    for k in range(4):
        spread = jnp.where(lanes == k, gates[:, k : k + 1] * (dgate[k] - mean), spread)
    dlogit_ref[...] = spread.T[:4, :]


def unpack(targets, gates, cotangent, returned):
    return pl.pallas_call(
        unpack_kernel,
        out_shape=(
            jax.ShapeDtypeStruct(cotangent.shape, BF),
            jax.ShapeDtypeStruct(gates.shape[::-1], F32),
        ),
        compiler_params=pltpu.CompilerParams(vmem_limit_bytes=16 << 20),
    )(targets, gates, cotangent, returned)


def gate_kernel(columns, *refs):
    dlogits, tokens, term_ref = refs[:-2], refs[-2], refs[-1]
    height = dlogits[0].shape[1]
    wide = lax.broadcasted_iota(jnp.int32, (term_ref.shape[1], height), 0)
    spreads = []
    for number, dlogit in enumerate(dlogits):
        spread = jnp.zeros(wide.shape, F32)
        for k in range(4):
            column = columns[k : k + 1, number * height : (number + 1) * height]
            spread = spread + jnp.where(column == wide, dlogit[k : k + 1, :], 0.0)
        spreads.append(spread)
    spread = jnp.concatenate(spreads, axis=1)
    total = 0.0
    for _ in range(3):
        piece = spread.astype(BF)
        spread = spread - piece.astype(F32)
        total = total + lax.dot_general(
            tokens[...], piece, TURNED_RIGHT, preferred_element_type=F32
        )
    term_ref[...] = total.astype(BF)


def gate_term(columns, dlogits, tokens, width):
    return pl.pallas_call(
        gate_kernel,
        out_shape=jax.ShapeDtypeStruct((tokens.shape[0], width), BF),
        compiler_params=pltpu.CompilerParams(vmem_limit_bytes=16 << 20),
    )(columns, *dlogits, tokens)


def exchange(values):
    return lax.all_to_all(values, "expert", split_axis=0, concat_axis=0, tiled=True)


def body(
    tokens,
    cotangent,
    domain_ids,
    shared_ids,
    private_ids,
    gate_weight,
    shared_in,
    shared_out,
    private_in,
    private_out,
):
    height, features = tokens.shape
    columns_all = DOMAINS * GATES
    n_batch = lax.axis_size("batch")
    me = lax.axis_index("batch")
    weights = (shared_in[0], private_in[0], shared_out[0], private_out[0])

    targets, packed = pack(domain_ids, shared_ids, private_ids, tokens)
    base = domain_ids[:, None] * GATES
    columns = jnp.concatenate([base + shared_ids, base + SHARED + private_ids], axis=1)
    targets, packed, tokens = lax.optimization_barrier((targets, packed, tokens))
    got = exchange(packed.reshape(-1, 2 * CAP, features))
    cells = jnp.arange(packed.shape[0], dtype=jnp.int32)
    picks = [cells[:, None] == targets[None, k, :] for k in range(4)]
    placed = (picks[0] | picks[1] | picks[2] | picks[3]).astype(BF)

    table = jnp.dot(
        tokens, gate_weight.reshape(features, columns_all), preferred_element_type=F32
    )
    every = jnp.arange(columns_all, dtype=jnp.int32)
    logits = jnp.sum(
        jnp.where(columns[:, :, None] == every[None, None, :], table[:, None, :], 0.0), axis=2
    )
    gates = jax.nn.softmax(logits, axis=1)
    columns, gates = lax.optimization_barrier((columns, gates))
    weight = sum(
        jnp.where(pick, gates[None, :, number], 0.0) for number, pick in enumerate(picks)
    )
    weight = jnp.sum(weight, axis=1, keepdims=True)
    spot = jnp.dot(placed, cotangent, preferred_element_type=F32)
    scaled = (weight * spot).astype(BF)

    width = features // n_batch
    columns_t = columns.T
    column_set = [columns_t]
    token_set = [lax.dynamic_slice_in_dim(tokens, me * width, width, axis=1)]
    for step in range(1, n_batch):
        to = (me + step) % n_batch
        token_set.append(turn(lax.dynamic_slice_in_dim(tokens, to * width, width, axis=1), step))
        column_set.append(turn(columns_t, step))
    token_part = jnp.concatenate(token_set, axis=0).T
    column_part = jnp.concatenate(column_set, axis=1)

    got, scaled, gates, targets, token_part, column_part = lax.optimization_barrier(
        (got, scaled, gates, targets.T, token_part, column_part)
    )

    own = by_kind(got.reshape(-1, features))
    near = near_blocks(own)
    pre_own, part_own = forward(own, (0, 1), weights)
    scaled, part_own[0] = lax.optimization_barrier((scaled, part_own[0]))
    near[0], near[3], part_own[1] = lax.optimization_barrier((near[0], near[3], part_own[1]))
    far = far_blocks(near)
    first = lax.optimization_barrier((near[0], near[3], near[1], near[2]))
    near[1], near[2] = first[2:]
    pre_first, part_first = forward(first[:2], (0, 1), weights)
    far[0], part_first[0] = lax.optimization_barrier((far[0], part_first[0]))
    scaled = exchange(scaled.reshape(-1, 2 * CAP, features))
    pre_far, part_far = forward(far, (0, 1), weights)
    pre_second, part_second = forward((near[1], near[2]), (1, 0), weights)
    part_near = (part_first[0], part_second[0], part_second[1], part_first[1])
    pre_near = (pre_first[0], pre_second[0], pre_second[1], pre_first[1])
    scaled, summed = scatter_ring(part_own, part_near, part_far, scaled)
    sent_own = by_kind(scaled.reshape(-1, features))
    ordered = [
        (o[0], n[0], n[2], f[0], o[1], n[1], n[3], f[1])
        for o, n, f in ((own, near, far), (pre_own, pre_near, pre_far))
    ]
    summed, sent_own, ordered = lax.optimization_barrier((summed, sent_own, ordered))
    sent_near = near_blocks(sent_own)
    returned = exchange(summed.reshape(-1, 2 * CAP, features)).reshape(-1, features)
    prepared = prepare(*ordered)
    prepared, sent_near[0] = lax.optimization_barrier((prepared, sent_near[0]))
    sent_far = far_blocks(sent_near)
    returned, sent_near = lax.optimization_barrier((returned, sent_near))

    mixed, dlogit = unpack(targets, gates, cotangent, returned)

    dlogit_set = [dlogit] + [turn(dlogit, step) for step in range(1, n_batch)]
    term = gate_term(column_part, dlogit_set, token_part, columns_all)
    pieces = term.reshape(-1, features // (n_batch * lax.axis_size("expert")), columns_all)
    grad_gate = jnp.sum(exchange(pieces).astype(F32), axis=0).reshape(-1, DOMAINS, GATES)

    o, n, f = sent_own, sent_near, sent_far
    sent = (o[0], n[0], n[2], f[0], o[1], n[1], n[3], f[1])
    grads = backward(prepared, sent, shared_out[0], private_out[0])
    return (mixed, *grads, grad_gate)


def solution(mesh):
    return jax.shard_map(
        body,
        mesh=mesh,
        in_specs=(
            P(("batch", "expert"), None),
            P(("batch", "expert"), None),
            P(("batch", "expert")),
            P(("batch", "expert"), None),
            P(("batch", "expert"), None),
            P(),
            P("expert", None, "batch"),
            P("expert", "batch", None),
            P("expert", None, "batch"),
            P("expert", "batch", None),
        ),
        out_specs=(
            P(("batch", "expert"), None),
            P("expert", None, "batch"),
            P("expert", "batch", None),
            P("expert", None, "batch"),
            P("expert", "batch", None),
            P(("batch", "expert"), None, None),
        ),
        check_vma=False,
    )
```
